32 devices in a mesh: groups: 2 (over y), lat: 4 (over z), chan: 2 (over x), pair: 2 (over core).
Axes of the slice: x: 2, y: 2, z: 4, core: 2. Of those that a mesh axis runs over, the one named last changes fastest.
Arguments:
- atmosphere: bfloat16 [512, 64, 1440], P('chan', ('groups', 'lat'), 'pair'), parts along dimension 1, may hold values from -6 to 6
- ocean_state: bfloat16 [256, 16384], P('chan', ('groups', 'lat', 'pair')), parts along dimension 1, may hold values from -6 to 6
- conv_taps: bfloat16 [512, 9], P('chan'), may hold values from -1.5 to 1.5
- atmos_gain: float32 [512], replicated, may hold values from 0.1 to 1.9
- atmos_up: bfloat16 [2048, 512], P('chan'), may hold values from -0.25 to 0.25
- atmos_down: bfloat16 [2048, 512], P('chan'), may hold values from -0.125 to 0.125
- ocean_gain: float32 [256], replicated, may hold values from 0.1 to 1.9
- ocean_up: bfloat16 [1024, 256], P('chan'), may hold values from -0.375 to 0.375
- ocean_down: bfloat16 [1024, 256], P('chan'), may hold values from -0.1875 to 0.1875
- remap_blocks: bfloat16 [64, 128, 128], replicated, may hold values from 0 to 4
- flux_sends: int32 [8, 8, 8], P(('lat', 'pair')), may hold values from 0 to 44
- flux_pattern: int32 [8, 128, 3], P(('lat', 'pair')), may hold values from 0 to 63, as said below
- sea_sends: int32 [8, 8, 1], P(('lat', 'pair')), may hold values from 0 to 7
- sea_pattern: int32 [8, 16, 3], P(('lat', 'pair')), may hold values from 0 to 63, as said below
- ocean_mask: int32 [64], P(('lat', 'pair')), may hold values 0 or 1
Outputs:
- atmos_next: bfloat16 [512, 64, 1440], P('chan', ('groups', 'lat'), 'pair'), parts along dimension 1
- ocean_next: bfloat16 [256, 16384], P('chan', ('groups', 'lat', 'pair')), parts along dimension 1
The draws below stay inside these ranges and needn't reach their ends.
There are 2 independent parts, one for each index of `groups`. The reference program is written for one: setup_inputs(seed, part) draws one part's arguments, and reference() takes and returns one part's arrays. A program takes and returns all parts, laid end to end along the dimension named above; an argument that names none is the same for every part. Nothing has to cross between parts.
Inputs may be any that keep to these rules, and one draw needn't show every extreme that they name: `flux_pattern`: on each peer every slot number below 64 appears exactly twice in column 0; column 1 is an ocean tile below 8, column 2 a block below 64. `sea_pattern`: on each peer every slot number below 8 appears exactly twice in column 0; column 1 is an atmosphere tile below 45, column 2 a block below 64.
All inputs are finite; a program needn't handle non-finite values. No bound on the sum of `ocean_mask` on one device may be relied on, other than what follows from the above.
Results may differ from the reference program's by a relative error of at most 0.0085.
Values may be sent and summed in bfloat16 or wider, within the bound.
No kernel may reach another device: no remote copies, remote signals or barrier semaphores. Data moves between devices by JAX's collectives and lax.ppermute only.
A program may use at most 128 MiB of HBM per device.

```python
import jax
import jax.numpy as jnp
from jax import lax

C = 512
OC = 256
HID = 2048
OHID = 1024
LON = 1440
A_ROWS = 8
O_TILES = 8
FLUX_CAP = 8
SEA_CAP = 1
BLOCKS = 64
PEERS = 8
LAT = 32
A_TILES = 45
OCELLS = 8192
N_LAT = 4
N_PAIR = 2


def pattern_rows(key, slot_count, tile_count):
    peer_keys = jax.random.split(key, PEERS)

    def one_peer(peer_key):
        key_first, key_second, key_tiles, key_blocks = jax.random.split(peer_key, 4)
        slot_order = jnp.concatenate([jax.random.permutation(key_first, slot_count), jax.random.permutation(key_second, slot_count)])
        target = jax.random.randint(key_tiles, (2 * slot_count,), 0, tile_count)
        target = target.at[1].set(tile_count - 1)
        chosen = jax.random.randint(key_blocks, (2 * slot_count,), 0, BLOCKS)
        chosen = chosen.at[0].set(BLOCKS - 1)
        return jnp.stack([slot_order.astype(jnp.int32), target.astype(jnp.int32), chosen.astype(jnp.int32)], axis=1)
    return jax.vmap(one_peer)(peer_keys)


def draw_flux_pattern(key, part):
    key = jax.random.fold_in(key, 17)
    return pattern_rows(key, PEERS * FLUX_CAP, O_TILES)


def draw_sea_pattern(key, part):
    key = jax.random.fold_in(key, 29)
    return pattern_rows(key, PEERS * SEA_CAP, A_TILES)


def draw_remap_blocks(key, part):
    key = jax.random.fold_in(key, 41)
    key_diagonal, key_spread = jax.random.split(key, 2)
    diagonal = jax.random.uniform(key_diagonal, (BLOCKS, 128), jnp.float32, 0.5, 1.5)
    spread = jax.random.uniform(key_spread, (BLOCKS, 128, 128), jnp.float32, 0.0, 1.0) / 128.0
    identity = jnp.eye(128, dtype=jnp.float32)
    result = identity[None, :, :] * diagonal[:, :, None] + spread
    return result.astype(jnp.bfloat16)


def touch_ends(values, stream_key, smallest, top_value):
    extent = values.shape
    spot = [jax.random.randint(jax.random.fold_in(stream_key, axis), (), 0, extent[axis]) for axis in range(len(extent))]
    values = values.at[tuple(spot)].set(smallest)
    longest = extent.index(max(extent))
    spot[longest] = (spot[longest] + 1) % extent[longest]
    return values.at[tuple(spot)].set(top_value)


def block_scale(rng, shape, cuts, least, top_value):
    factor_of = 1.0
    for position, parts in cuts:
        steps = jax.random.uniform(jax.random.fold_in(jax.random.fold_in(rng, 6), position), (parts,), jnp.float32, least / len(cuts), top_value / len(cuts))
        factor_of = factor_of * jnp.repeat(jnp.exp(steps), shape[position] // parts).reshape((-1,) + (1,) * (len(shape) - 1 - position))
    return factor_of


def bell_draw(own_key, dims, scale, most, pieces=(), held_as=jnp.bfloat16):
    gain = block_scale(own_key, dims, pieces, -0.22, 0.18) if pieces else 1.0
    values = jax.random.normal(own_key, dims, jnp.float32) * scale * gain
    return jnp.minimum(jnp.maximum(values, -most), most).astype(held_as)


def setup_inputs(seed: int = 0, part: int = 0) -> dict:
    streams_of = jax.random.split(jax.random.key(seed), 16)
    own_keys = jax.random.split(jax.random.fold_in(streams_of[15], part), 16)
    atmosphere = bell_draw(own_keys[0], (C, LAT, LON), 1.0, 6.0, ((0, 2), (1, 4), (2, 2)))
    ocean_state = bell_draw(own_keys[1], (OC, OCELLS), 1.0, 6.0, ((0, 2), (1, 8)))
    conv_taps = bell_draw(streams_of[2], (C, 9), 0.3, 1.5, ((0, 2),))
    atmos_gain = jnp.clip(1.0 + 0.18 * jax.random.normal(streams_of[3], (C,), jnp.float32), 0.1, 1.9)
    atmos_up = bell_draw(streams_of[4], (HID, C), C ** -0.5, 0.25, ((0, 2),))
    atmos_down = bell_draw(streams_of[5], (HID, C), HID ** -0.5, 0.125, ((0, 2),))
    ocean_gain = jnp.clip(1.0 + 0.18 * jax.random.normal(streams_of[6], (OC,), jnp.float32), 0.1, 1.9)
    ocean_up = bell_draw(streams_of[7], (OHID, OC), OC ** -0.5, 0.375, ((0, 2),))
    ocean_down = bell_draw(streams_of[8], (OHID, OC), OHID ** -0.5, 0.1875, ((0, 2),))
    remap_blocks = draw_remap_blocks(jax.random.fold_in(streams_of[15], 71), part)
    flux_sends = touch_ends(jax.random.randint(streams_of[10], (PEERS, PEERS, FLUX_CAP), 0, A_TILES), jax.random.fold_in(streams_of[10], 1), 0, A_TILES - 1).astype(jnp.int32)
    flux_pattern = draw_flux_pattern(jax.random.fold_in(streams_of[15], 71), part)
    sea_sends = touch_ends(jax.random.randint(streams_of[12], (PEERS, PEERS, SEA_CAP), 0, O_TILES), jax.random.fold_in(streams_of[12], 1), 0, O_TILES - 1).astype(jnp.int32)
    sea_pattern = draw_sea_pattern(jax.random.fold_in(streams_of[15], 71), part)
    ocean_mask = touch_ends((jax.random.randint(streams_of[14], (OCELLS // 128,), 0, 4) < 3).astype(jnp.int32), jax.random.fold_in(streams_of[14], 1), 0, 1)
    return {"atmosphere": atmosphere, "ocean_state": ocean_state, "conv_taps": conv_taps, "atmos_gain": atmos_gain, "atmos_up": atmos_up, "atmos_down": atmos_down, "ocean_gain": ocean_gain, "ocean_up": ocean_up, "ocean_down": ocean_down, "remap_blocks": remap_blocks, "flux_sends": flux_sends, "flux_pattern": flux_pattern, "sea_sends": sea_sends, "sea_pattern": sea_pattern, "ocean_mask": ocean_mask}


def atmos_tiles(field):
    depth = field.shape[0]
    half_width = LON // N_PAIR
    blocked = field.reshape(depth, N_LAT, A_ROWS, N_PAIR, half_width)
    blocked = blocked.transpose(1, 3, 0, 2, 4)
    return blocked.reshape(N_LAT * N_PAIR, depth, A_ROWS * half_width // 128, 128)

def atmos_field(tiles):
    depth = tiles.shape[1]
    half_width = LON // N_PAIR
    blocked = tiles.reshape(N_LAT, N_PAIR, depth, A_ROWS, half_width)
    return blocked.transpose(2, 0, 3, 1, 4).reshape(depth, N_LAT * A_ROWS, LON)

def remap_all(sources, sends, pattern, blocks, tile_count, factor):
    slot_count = sends.shape[2]
    targets = jnp.arange(tile_count, dtype=jnp.int32)

    def one_peer(target):
        entries = pattern[target]
        slot_index = entries[:, 0]
        source = slot_index // slot_count
        within = slot_index % slot_count
        column = sends[:, target, :]
        tile_index = column[source, within]
        picked = sources[source, :, tile_index, :]
        weights = blocks[entries[:, 2]].astype(jnp.float32)
        products = jnp.einsum('eki,eij->ekj', picked, weights)
        onehot = (entries[:, 1][:, None] == targets[None, :]).astype(jnp.float32)
        return jnp.einsum('ekj,et->ktj', products, onehot) * factor
    return lax.map(one_peer, jnp.arange(sources.shape[0], dtype=jnp.int32))

def normalize(values, channel_gain):
    widened = values.astype(jnp.float32)
    inverse = lax.rsqrt(lax.optimization_barrier(jnp.mean(widened * widened, axis=0, keepdims=True)) + 1e-06)
    return (widened * inverse * channel_gain[:, None]).astype(jnp.bfloat16)

def feed_forward(values, channel_gain, up_weight, down_weight):
    normed = normalize(values, channel_gain)
    hidden = jax.nn.gelu(jnp.dot(up_weight, normed, preferred_element_type=jnp.float32)).astype(jnp.bfloat16)
    return lax.dot_general(down_weight, hidden, (((0,), (0,)), ((), ())), preferred_element_type=jnp.float32)

def reference(atmosphere, ocean_state, conv_taps, atmos_gain, atmos_up, atmos_down, ocean_gain, ocean_up, ocean_down, remap_blocks, flux_sends, flux_pattern, sea_sends, sea_pattern, ocean_mask):
    peer_count = N_LAT * N_PAIR
    channels, lat_total, lon_total = atmosphere.shape
    ocean_depth = ocean_state.shape[0]
    flux_sources = atmos_tiles(atmosphere[0::2].astype(jnp.float32))
    ocean_sources = ocean_state.astype(jnp.float32).reshape(ocean_depth, peer_count, O_TILES, 128).transpose(1, 0, 2, 3)
    flux_ocean = remap_all(flux_sources, flux_sends, flux_pattern, remap_blocks, O_TILES, 0.125)
    flux_ocean = flux_ocean.transpose(1, 0, 2, 3).reshape(ocean_depth, peer_count * O_TILES * 128)
    sea_atmos = atmos_field(remap_all(ocean_sources, sea_sends, sea_pattern, remap_blocks, A_TILES, 1.0))
    state = atmosphere.astype(jnp.float32)
    padded = jnp.pad(state, ((0, 0), (1, 1), (0, 0)))
    padded = jnp.concatenate([padded[:, :, -1:], padded, padded[:, :, :1]], axis=2)
    tap_table = conv_taps.astype(jnp.float32)
    smooth = jnp.zeros_like(state)
    for row_step in range(3):
        for col_step in range(3):
            smooth = smooth + tap_table[:, 3 * row_step + col_step][:, None, None] * padded[:, row_step:row_step + lat_total, col_step:col_step + lon_total]
    combined = state + smooth
    combined = combined.at[1::2].add(sea_atmos)
    atmos_input = combined.astype(jnp.bfloat16)
    ocean_input = (ocean_state.astype(jnp.float32) + flux_ocean).astype(jnp.bfloat16)

    def atmos_row(row_values):
        delta = feed_forward(row_values, atmos_gain, atmos_up, atmos_down)
        return (row_values.astype(jnp.float32) + delta).astype(jnp.bfloat16)
    atmos_next = lax.map(atmos_row, atmos_input.transpose(1, 0, 2)).transpose(1, 0, 2)
    ocean_blocks = ocean_input.reshape(ocean_depth, peer_count, O_TILES * 128).transpose(1, 0, 2)
    mask_blocks = jnp.repeat(ocean_mask.astype(jnp.float32), 128).reshape(peer_count, O_TILES * 128)

    def ocean_block(pair_values):
        block_values, block_mask = pair_values
        delta = feed_forward(block_values, ocean_gain, ocean_up, ocean_down)
        return (block_values.astype(jnp.float32) + block_mask[None, :] * delta).astype(jnp.bfloat16)
    ocean_next = lax.map(ocean_block, (ocean_blocks, mask_blocks)).transpose(1, 0, 2).reshape(ocean_depth, peer_count * O_TILES * 128)
    return (atmos_next, ocean_next)
```

```python
import functools
import math

import jax
import jax.numpy as jnp
from jax import lax
from jax.experimental import pallas as pl
from jax.experimental.pallas import tpu as pltpu
from jax.sharding import PartitionSpec as P


def padded_2(block, sides, width):
    for axis, dim in sides:
        count = lax.axis_size(axis)
        forward = [(i, i + 1) for i in range(count - 1)]
        forward.append((count - 1, 0))
        backward = [(target, source) for source, target in forward]
        low = lax.ppermute(
            lax.slice_in_dim(block, block.shape[dim] - width, None, axis=dim), axis, forward
        )
        high = lax.ppermute(lax.slice_in_dim(block, 0, width, axis=dim), axis, backward)
        block = jnp.concatenate([low, block, high], axis=dim)
    return block


def remap_tiles(received, pattern, blocks, tile_count, factor):
    flux_depth = received.shape[0]
    entries = pattern.shape[0]
    group_size = math.gcd(entries, 64)
    grouped = pattern.reshape(entries // group_size, group_size, 3)
    targets = jnp.arange(tile_count, dtype=jnp.int32)

    def add_group(running, entry_rows):
        picked = jnp.take(received, entry_rows[:, 0], axis=1)
        weights = jnp.take(blocks, entry_rows[:, 2], axis=0)
        products = jnp.einsum("kgi,gij->kgj", picked, weights, preferred_element_type=jnp.float32)
        onehot = (entry_rows[:, 1][:, None] == targets[None, :]).astype(jnp.float32)
        return (running + jnp.einsum("kgj,gt->ktj", products, onehot), None)

    initial = jnp.zeros((flux_depth, tile_count, 128), jnp.float32)
    summed, _ = lax.scan(add_group, initial, grouped)
    return summed * factor


def normalize(values, channel_gain):
    widened = values.astype(jnp.float32)
    inverse = lax.rsqrt(jnp.mean(widened * widened, axis=0, keepdims=True) + 1e-06)
    return (widened * inverse * channel_gain[:, None]).astype(jnp.bfloat16)


def shards(
    atmosphere,
    ocean_state,
    conv_taps,
    atmos_gain,
    atmos_up,
    atmos_down,
    ocean_gain,
    ocean_up,
    ocean_down,
    remap_blocks,
    flux_sends,
    flux_pattern,
    sea_sends,
    sea_pattern,
    ocean_mask,
):
    lat_bands = lax.axis_size("lat")
    halves = lax.axis_size("pair")
    peer_count = lat_bands * halves
    channels, lat_rows, lon_cells = atmosphere.shape
    flux_depth, ocean_cells = ocean_state.shape
    atmos_count = lat_rows * lon_cells // 128
    ocean_count = ocean_cells // 128
    flux_slots = flux_sends.shape[2]
    sea_slots = sea_sends.shape[2]
    flux_tiles = atmosphere[0::2].reshape(flux_depth, atmos_count, 128)
    ocean_tiles = ocean_state.reshape(flux_depth, ocean_count, 128)
    flux_out = jnp.take(flux_tiles, flux_sends[0].reshape(-1), axis=1)
    sea_out = jnp.take(ocean_tiles, sea_sends[0].reshape(-1), axis=1)
    flux_in, sea_in = (
        lax.all_to_all(
            flux_out.reshape(flux_depth, peer_count, flux_slots, 128),
            ("lat", "pair"),
            split_axis=1,
            concat_axis=1,
            tiled=True,
        ),
        lax.all_to_all(
            sea_out.reshape(flux_depth, peer_count, sea_slots, 128),
            ("lat", "pair"),
            split_axis=1,
            concat_axis=1,
            tiled=True,
        ),
    )
    flux_in = flux_in.reshape(flux_depth, peer_count * flux_slots, 128)
    sea_in = sea_in.reshape(flux_depth, peer_count * sea_slots, 128)
    flux_ocean = remap_tiles(flux_in, flux_pattern[0], remap_blocks, ocean_count, 0.125)
    sea_atmos = remap_tiles(sea_in, sea_pattern[0], remap_blocks, atmos_count, 1.0)
    ocean_input = (
        ocean_state.astype(jnp.float32) + flux_ocean.reshape(flux_depth, ocean_cells)
    ).astype(jnp.bfloat16)
    padded = padded_2(atmosphere, (("lat", 1), ("pair", 2)), 1)
    lat_index = lax.axis_index("lat")
    edge_rows = jnp.arange(lat_rows + 2)
    row_keep = ((edge_rows > 0) | (lat_index > 0)) & (
        (edge_rows < lat_rows + 1) | (lat_index < lat_bands - 1)
    )
    padded = padded.astype(jnp.float32) * row_keep.astype(jnp.float32)[None, :, None]
    tap_table = conv_taps.astype(jnp.float32)
    smooth = jnp.zeros((channels, lat_rows, lon_cells), jnp.float32)
    for row_step in range(3):
        for col_step in range(3):
            smooth = (
                smooth
                + tap_table[:, 3 * row_step + col_step][:, None, None]
                * padded[:, row_step : row_step + lat_rows, col_step : col_step + lon_cells]
            )
    combined = atmosphere.astype(jnp.float32) + smooth
    combined = combined.at[1::2].add(sea_atmos.reshape(flux_depth, lat_rows, lon_cells))
    atmos_input = combined.astype(jnp.bfloat16)
    atmos_cells, ocean_part = (
        lax.all_to_all(
            atmos_input.reshape(channels, lat_rows * lon_cells),
            "chan",
            split_axis=1,
            concat_axis=0,
            tiled=True,
        ),
        lax.all_to_all(ocean_input, "chan", split_axis=1, concat_axis=0, tiled=True),
    )
    atmos_normed = normalize(atmos_cells, atmos_gain)
    ocean_normed = normalize(ocean_part, ocean_gain)
    up_rows = lax.all_gather(atmos_up, "chan", axis=0, tiled=True)
    down_rows = lax.all_gather(atmos_down, "chan", axis=0, tiled=True)
    ocean_up_rows = lax.all_gather(ocean_up, "chan", axis=0, tiled=True)
    ocean_down_rows = lax.all_gather(ocean_down, "chan", axis=0, tiled=True)
    hidden = jax.nn.gelu(jnp.dot(up_rows, atmos_normed, preferred_element_type=jnp.float32)).astype(
        jnp.bfloat16
    )
    atmos_sum = lax.dot_general(
        down_rows, hidden, (((0,), (0,)), ((), ())), preferred_element_type=jnp.float32
    )
    ocean_hidden = jax.nn.gelu(
        jnp.dot(ocean_up_rows, ocean_normed, preferred_element_type=jnp.float32)
    ).astype(jnp.bfloat16)
    ocean_sum = lax.dot_general(
        ocean_down_rows, ocean_hidden, (((0,), (0,)), ((), ())), preferred_element_type=jnp.float32
    )
    ocean_stretch = ocean_part.shape[1]
    mask_cells = jnp.repeat(ocean_mask.astype(jnp.float32), 128)
    mask_cells = lax.dynamic_slice_in_dim(
        mask_cells, lax.axis_index("chan") * ocean_stretch, ocean_stretch
    )
    atmos_after = (atmos_cells.astype(jnp.float32) + atmos_sum).astype(jnp.bfloat16)
    ocean_after = (ocean_part.astype(jnp.float32) + mask_cells[None, :] * ocean_sum).astype(
        jnp.bfloat16
    )
    atmos_back, ocean_back = (
        lax.all_to_all(atmos_after, "chan", split_axis=0, concat_axis=1, tiled=True),
        lax.all_to_all(ocean_after, "chan", split_axis=0, concat_axis=1, tiled=True),
    )
    return (atmos_back.reshape(channels, lat_rows, lon_cells), ocean_back)


SWAP = [(0, 1), (1, 0)]
LIMIT = 56 * 1024 * 1024


def vmem():
    return pl.BlockSpec(memory_space=pltpu.VMEM)


def smem():
    return pl.BlockSpec(memory_space=pltpu.SMEM)


def local_call(body, out_shape, operands, in_specs, out_specs, scratch=(), flops=0, moved=0, exps=0, aliases=None):
    return pl.pallas_call(
        body,
        grid=(1,),
        out_shape=out_shape,
        in_specs=in_specs,
        out_specs=out_specs,
        scratch_shapes=list(scratch),
        input_output_aliases=aliases or {},
        compiler_params=pltpu.CompilerParams(vmem_limit_bytes=LIMIT),
        cost_estimate=pl.CostEstimate(flops=flops, bytes_accessed=moved, transcendentals=exps),
    )(*operands)


def sea_pick_body(sends, ocean, out):
    count, cap = sends.shape
    for peer in range(count):
        for slot in range(cap):
            at = pl.multiple_of(sends[peer, slot] * 128, 128)
            out[peer * cap + slot] = ocean[:, pl.ds(at, 128)]


def flux_pick_body(sends, cells, pick, out, even):
    count, cap = sends.shape
    step = cells.shape[0] // 15
    for block in range(15):
        rows = pl.ds(block * step, step)
        even[rows, :] = jnp.dot(
            cells[rows, :], pick[...], preferred_element_type=jnp.float32
        ).astype(jnp.bfloat16)

    def one_peer(peer, carry):
        for slot in range(cap):
            at = pl.multiple_of(sends[peer, slot] * 128, 128)
            out[peer * cap + slot] = even[pl.ds(at, 128), :]
        return carry

    lax.fori_loop(0, count, one_peer, 0)


def sea_products_body(pattern, slots, blocks, spread, out, wide):
    def widen(slot, carry):
        wide[slot] = lax.dot_general(
            slots[slot], spread[...], (((0,), (0,)), ((), ())), preferred_element_type=jnp.float32
        ).astype(jnp.bfloat16)
        return carry

    lax.fori_loop(0, slots.shape[0], widen, 0, unroll=4)

    def entry(index, carry):
        out[index] = lax.dot_general(
            blocks[pattern[index, 2]],
            wide[pattern[index, 0]],
            (((0,), (0,)), ((), ())),
            preferred_element_type=jnp.float32,
        )
        return carry

    lax.fori_loop(0, out.shape[0], entry, 0, unroll=4)


def smooth_body(first_row, edge_low, edge_high, pattern, *refs):
    rows, (sides, taps, sea, out, padded, total) = refs[:4], refs[4:]
    cells = out.shape[1]
    for place in range(4):
        at_edge = (place == 0 and edge_low) or (place == 3 and edge_high)
        for half in range(2):
            lanes = slice(half * 128, half * 128 + 128)
            padded[half, place, 8 : 8 + cells, :] = rows[place][0, 0:cells, lanes].astype(jnp.float32)
            if at_edge:
                pair = rows[place][0, cells : cells + 16, lanes].astype(jnp.float32)
                left, right = pair[0:1], pair[1:2]
            else:
                at = 2 * (first_row - 1 + place)
                pair = sides[:, lanes].astype(jnp.float32)
                left, right = pair[at : at + 1], pair[at + 1 : at + 2]
            padded[half, place, 7:8, :] = left
            padded[half, place, 8 + cells : 9 + cells, :] = right
    block = 80 if cells % 80 == 0 else 16
    for half in range(2):
        lanes = slice(half * 128, half * 128 + 128)
        scale = [taps[k : k + 1, lanes] for k in range(9)]
        for row in range(2):
            for base in range(0, cells, block):
                value = padded[half, row + 1, 8 + base : 8 + base + block, :] * (scale[4] + 1.0)
                for k in (0, 1, 2, 3, 5, 6, 7, 8):
                    start = 7 + base + k % 3
                    value = value + scale[k] * padded[half, row + k // 3, start : start + block, :]
                start = 128 + row * cells + base
                total[start : start + block, lanes] = value
    span = 2 * cells
    for entry in range(sea.shape[0]):
        start = pattern[entry, 1] * 128 - first_row * cells + 128

        @pl.when((start > 0) & (start < span + 128))
        def _():
            where = pl.ds(pl.multiple_of(start, 16), 128)
            total[where, :] = total[where, :] + sea[entry]

    for row in range(2):
        out[row] = total[128 + row * cells : 128 + (row + 1) * cells, :].astype(jnp.bfloat16)


def gelu(v):
    inner = v * (0.7978845608028654 + 0.035677408136300125 * (v * v))
    half = 0.5 * v
    return half + half * jnp.tanh(inner)


def atmos_layer_body(chan, own, other, gain, up, down, *refs):
    pieces, out = refs[:4], refs[-1]
    width = own.shape[2]
    mine = pl.ds(pl.multiple_of(chan[0] * width, 128), width)
    theirs = pl.ds(pl.multiple_of((1 - chan[0]) * width, 128), width)
    depth = pieces[0].shape[0] * 4 // 5
    gain_mine, gain_theirs = gain[:, mine], gain[:, theirs]
    cells = own.shape[1]
    step = 360 if cells % 360 == 0 and 360 % 8 == 0 else 16
    step = 240

    def rows_step(index, carry):
        row = index // (cells // step)
        at = pl.ds(pl.multiple_of((index % (cells // step)) * step, 16), step)
        a = own[row, at, :].astype(jnp.float32)
        b = other[row, at, :].astype(jnp.float32)
        squares = jnp.sum(a * a + b * b, axis=1, keepdims=True)
        inverse = lax.rsqrt(squares * (1.0 / (2 * width)) + 1e-06)
        na = (a * inverse * gain_mine).astype(jnp.bfloat16)
        nb = (b * inverse * gain_theirs).astype(jnp.bfloat16)
        total = a
        nt = (((1,), (1,)), ((), ()))
        for part in range(8):
            if part < 4:
                where = slice(part * depth, (part + 1) * depth)
                ua, ub, d = up[where, mine], up[where, theirs], down[where, mine]
            else:
                piece = pieces[part - 4]
                ua, ub = piece[0:depth, mine], piece[0:depth, theirs]
                d = piece[0:depth, 2 * width : 3 * width]
            v = lax.dot_general(na, ua, nt, preferred_element_type=jnp.float32)
            v = v + lax.dot_general(nb, ub, nt, preferred_element_type=jnp.float32)
            hidden = gelu(v).astype(jnp.bfloat16)
            total = total + jnp.dot(hidden, d, preferred_element_type=jnp.float32)
        out[row, at, :] = total.astype(jnp.bfloat16)
        return carry

    lax.fori_loop(0, own.shape[0] * (cells // step), rows_step, 0)


def flux_remap_body(pattern, slots, blocks, ocean, out, total):
    total[...] = jnp.zeros_like(total)

    def entry(index, carry):
        tile = pattern[index, 1]
        total[tile] = total[tile] + lax.dot_general(
            slots[pattern[index, 0]],
            blocks[pattern[index, 2]],
            (((0,), (0,)), ((), ())),
            preferred_element_type=jnp.float32,
        )
        return carry

    lax.fori_loop(0, pattern.shape[0], entry, 0, unroll=8)
    for tile in range(total.shape[0]):
        lanes = slice(tile * 128, tile * 128 + 128)
        out[:, lanes] = (ocean[:, lanes].astype(jnp.float32) + 0.125 * total[tile]).astype(jnp.bfloat16)


def ocean_layer_body(chan, mask, own, other, gain, up, down, *refs):
    pieces, out = refs[:4], refs[-1]
    width = own.shape[0]
    mine = pl.ds(pl.multiple_of(chan[0] * width, 128), width)
    theirs = pl.ds(pl.multiple_of((1 - chan[0]) * width, 128), width)
    depth = pieces[0].shape[0] // 5
    top = 4 * depth
    gain_mine, gain_theirs = gain[mine, :], gain[theirs, :]
    a = own[...].astype(jnp.float32)
    b = other[...].astype(jnp.float32)
    squares = jnp.sum(a * a + b * b, axis=0, keepdims=True)
    inverse = lax.rsqrt(squares * (1.0 / (2 * width)) + 1e-06)
    na = (a * inverse * gain_mine).astype(jnp.bfloat16)
    nb = (b * inverse * gain_theirs).astype(jnp.bfloat16)
    ups, downs = [(up[:, mine], up[:, theirs])], [down[:, mine]]
    for piece in pieces:
        for side in range(2):
            base = side * 3 * width
            left = piece[top:, pl.ds(pl.multiple_of(base + chan[0] * width, 128), width)]
            right = piece[top:, pl.ds(pl.multiple_of(base + (1 - chan[0]) * width, 128), width)]
            ups.append((left, right))
            downs.append(piece[top:, base + 2 * width : base + 3 * width])
    total = jnp.zeros_like(a)
    for (ua, ub), d in zip(ups, downs):
        v = jnp.dot(ua, na, preferred_element_type=jnp.float32)
        v = v + jnp.dot(ub, nb, preferred_element_type=jnp.float32)
        hidden = gelu(v).astype(jnp.bfloat16)
        total = total + lax.dot_general(
            d, hidden, (((0,), (0,)), ((), ())), preferred_element_type=jnp.float32
        )
    for tile in range(mask.shape[0]):
        lanes = slice(tile * 128, tile * 128 + 128)
        keep = mask[tile].astype(jnp.float32)
        out[:, lanes] = (a[:, lanes] + keep * total[:, lanes]).astype(jnp.bfloat16)


def far_weights(up, down, ocean_up, ocean_down):
    chan = lax.axis_index("chan")
    quarter = lax.axis_index("groups") * 2 + lax.axis_index("pair")
    depth, shallow = up.shape[0] // 4, ocean_up.shape[0] // 4
    width, narrow = up.shape[1] // 2, ocean_up.shape[1] // 2
    first = lax.dynamic_slice(up, (quarter * depth, 0), (depth, 2 * width))
    second = lax.dynamic_slice(down, (quarter * depth, (1 - chan) * width), (depth, width))
    third = lax.dynamic_slice(ocean_up, (quarter * shallow, 0), (shallow, 2 * narrow))
    fourth = lax.dynamic_slice(ocean_down, (quarter * shallow, (1 - chan) * narrow), (shallow, narrow))
    low = jnp.concatenate([third, fourth], axis=1)
    low = jnp.concatenate([low[: shallow // 2], low[shallow // 2 :]], axis=1)
    packed = jnp.concatenate([jnp.concatenate([first, second], axis=1), low], axis=0)
    one = lax.ppermute(packed, "chan", SWAP)
    two = lax.ppermute(one, "groups", SWAP)
    return one, two, lax.ppermute(one, "pair", SWAP), lax.ppermute(two, "pair", SWAP)


def quick_shards(
    atmosphere,
    ocean_state,
    conv_taps,
    atmos_gain,
    atmos_up,
    atmos_down,
    ocean_gain,
    ocean_up,
    ocean_down,
    remap_blocks,
    flux_sends,
    flux_pattern,
    sea_sends,
    sea_pattern,
    ocean_mask,
):
    bf16, f32 = jnp.bfloat16, jnp.float32
    channels, lat_rows, lon_cells = atmosphere.shape
    flux_depth, ocean_cells = ocean_state.shape
    ocean_count = ocean_cells // 128
    lat_bands = lax.axis_size("lat")
    peers = ("lat", "pair")
    chan = lax.axis_index("chan").reshape(1)
    field = atmosphere.transpose(1, 2, 0)
    pick = (jnp.arange(channels)[:, None] == 2 * jnp.arange(flux_depth)[None, :]).astype(bf16)
    spread = (2 * jnp.arange(flux_depth)[:, None] + 1 == jnp.arange(channels)[None, :]).astype(bf16)

    sends = sea_sends[0]
    sea_out = local_call(
        sea_pick_body,
        jax.ShapeDtypeStruct((sends.size, flux_depth, 128), bf16),
        (sends, ocean_state),
        [smem(), vmem()],
        vmem(),
        moved=2**20,
    )
    sea_in = lax.all_to_all(sea_out, peers, split_axis=0, concat_axis=0, tiled=True)

    sides = jnp.stack([field[:, lon_cells - 1, :], field[:, 0, :]], axis=1).reshape(2 * lat_rows, channels)
    sides = lax.ppermute(sides, "pair", SWAP)

    pieces = far_weights(atmos_up, atmos_down, ocean_up, ocean_down)

    fill = jnp.zeros((14, channels), bf16)
    up_chain = [(i, i + 1) for i in range(lat_bands - 1)]
    down_chain = [(i + 1, i) for i in range(lat_bands - 1)]
    low = lax.ppermute(jnp.concatenate([field[lat_rows - 1], sides[-2:], fill], axis=0), "lat", up_chain)
    high = lax.ppermute(jnp.concatenate([field[0], sides[:2], fill], axis=0), "lat", down_chain)

    sends = flux_sends[0]
    flux_out = local_call(
        flux_pick_body,
        jax.ShapeDtypeStruct((sends.size, 128, flux_depth), bf16),
        (sends, field.reshape(lat_rows * lon_cells, channels), pick),
        [smem(), vmem(), vmem()],
        vmem(),
        scratch=[pltpu.VMEM((lat_rows * lon_cells, flux_depth), bf16)],
        flops=2 * lat_rows * lon_cells * channels * flux_depth,
        moved=6 * 2**20,
    )
    flux_in = lax.all_to_all(flux_out, peers, split_axis=0, concat_axis=0, tiled=True)

    pattern = sea_pattern[0]
    sea = local_call(
        sea_products_body,
        jax.ShapeDtypeStruct((pattern.shape[0], 128, channels), f32),
        (pattern, sea_in, remap_blocks, spread),
        [smem(), vmem(), vmem(), vmem()],
        vmem(),
        scratch=[pltpu.VMEM((sea_in.shape[0], 128, channels), bf16)],
        flops=2 * pattern.shape[0] * 128 * 128 * channels,
        moved=4 * 2**20,
    )
    taps = conv_taps.T.astype(f32)

    def smooth_rows(first):
        operands, specs = [], []
        for row in range(first - 1, first + 3):
            if row < 0 or row >= lat_rows:
                operands.append((low if row < 0 else high)[None])
                specs.append(vmem())
            else:
                operands.append(field)
                specs.append(pl.BlockSpec((1, lon_cells, channels), lambda _, row=row: (row, 0, 0)))
        return local_call(
            functools.partial(smooth_body, first, first == 0, first + 2 == lat_rows),
            jax.ShapeDtypeStruct((2, lon_cells, channels), bf16),
            (pattern, *operands, sides, taps, sea),
            [smem(), *specs, vmem(), vmem(), vmem()],
            vmem(),
            scratch=[
                pltpu.VMEM((2, 4, lon_cells + 16, 128), f32),
                pltpu.VMEM((2 * lon_cells + 256, channels), f32),
            ],
            flops=36 * lon_cells * channels,
            moved=5 * 2**20,
        )

    order = [2, 4, 0, 6]
    inputs = [smooth_rows(first) for first in order]
    others = [lax.ppermute(value, "chan", SWAP) for value in inputs]

    pattern = flux_pattern[0]
    ocean_input = local_call(
        flux_remap_body,
        jax.ShapeDtypeStruct((flux_depth, ocean_cells), bf16),
        (pattern, flux_in, remap_blocks, ocean_state),
        [smem(), vmem(), vmem(), vmem()],
        vmem(),
        scratch=[pltpu.VMEM((ocean_count, flux_depth, 128), f32)],
        flops=2 * pattern.shape[0] * 128 * 128 * flux_depth,
        moved=5 * 2**20,
    )
    ocean_other = lax.ppermute(ocean_input, "chan", SWAP)

    result = None
    gain = atmos_gain.reshape(1, -1)
    for first, own, other in zip(order, inputs, others):
        operands = [chan, own, other, gain, atmos_up, atmos_down, *pieces]
        specs = [smem()] + [vmem()] * (len(operands) - 1)
        aliases = {}
        if result is not None:
            aliases = {len(operands): 0}
            operands.append(result)
            specs.append(pl.BlockSpec(memory_space=pl.ANY))
        result = local_call(
            atmos_layer_body,
            jax.ShapeDtypeStruct((lat_rows, lon_cells, channels), bf16),
            operands,
            specs,
            pl.BlockSpec((2, lon_cells, channels), lambda _, first=first: (first // 2, 0, 0)),
            flops=2 * 2 * lon_cells * 3 * channels * 2 * atmos_up.shape[0],
            moved=8 * 2**20,
            exps=2 * lon_cells * 2 * atmos_up.shape[0],
            aliases=aliases,
        )
    ocean_next = local_call(
        ocean_layer_body,
        jax.ShapeDtypeStruct((flux_depth, ocean_cells), bf16),
        (chan, ocean_mask, ocean_input, ocean_other, ocean_gain.reshape(-1, 1), ocean_up, ocean_down, *pieces),
        [smem(), smem()] + [vmem()] * 9,
        vmem(),
        flops=2 * ocean_cells * 3 * flux_depth * 2 * ocean_up.shape[0],
        moved=4 * 2**20,
        exps=ocean_cells * 2 * ocean_up.shape[0],
    )
    return result.transpose(2, 0, 1), ocean_next


def solution(mesh):
    in_specs = (
        P("chan", ("groups", "lat"), "pair"),
        P("chan", ("groups", "lat", "pair")),
        P("chan", None),
        P(),
        P("chan", None),
        P("chan", None),
        P(),
        P("chan", None),
        P("chan", None),
        P(),
        P(("lat", "pair"), None, None),
        P(("lat", "pair"), None, None),
        P(("lat", "pair"), None, None),
        P(("lat", "pair"), None, None),
        P(("lat", "pair")),
    )
    out_specs = (P("chan", ("groups", "lat"), "pair"), P("chan", ("groups", "lat", "pair")))
    paired = all(mesh.shape[axis] == 2 for axis in ("groups", "chan", "pair"))
    body = quick_shards if paired else shards
    return jax.shard_map(body, mesh=mesh, in_specs=in_specs, out_specs=out_specs, check_vma=False)
```

```python
import functools
import math

import jax
import jax.numpy as jnp
from jax import lax
from jax.experimental import pallas as pl
from jax.experimental.pallas import tpu as pltpu
from jax.sharding import PartitionSpec as P


def padded_2(block, sides, width):
    for axis, dim in sides:
        count = lax.axis_size(axis)
        forward = [(i, i + 1) for i in range(count - 1)]
        forward.append((count - 1, 0))
        backward = [(target, source) for source, target in forward]
        low = lax.ppermute(
            lax.slice_in_dim(block, block.shape[dim] - width, None, axis=dim), axis, forward
        )
        high = lax.ppermute(lax.slice_in_dim(block, 0, width, axis=dim), axis, backward)
        block = jnp.concatenate([low, block, high], axis=dim)
    return block


def remap_tiles(received, pattern, blocks, tile_count, factor):
    flux_depth = received.shape[0]
    entries = pattern.shape[0]
    group_size = math.gcd(entries, 64)
    grouped = pattern.reshape(entries // group_size, group_size, 3)
    targets = jnp.arange(tile_count, dtype=jnp.int32)

    def add_group(running, entry_rows):
        picked = jnp.take(received, entry_rows[:, 0], axis=1)
        weights = jnp.take(blocks, entry_rows[:, 2], axis=0)
        products = jnp.einsum("kgi,gij->kgj", picked, weights, preferred_element_type=jnp.float32)
        onehot = (entry_rows[:, 1][:, None] == targets[None, :]).astype(jnp.float32)
        return (running + jnp.einsum("kgj,gt->ktj", products, onehot), None)

    initial = jnp.zeros((flux_depth, tile_count, 128), jnp.float32)
    summed, _ = lax.scan(add_group, initial, grouped)
    return summed * factor


def normalize(values, channel_gain):
    widened = values.astype(jnp.float32)
    inverse = lax.rsqrt(jnp.mean(widened * widened, axis=0, keepdims=True) + 1e-06)
    return (widened * inverse * channel_gain[:, None]).astype(jnp.bfloat16)


def shards(
    atmosphere,
    ocean_state,
    conv_taps,
    atmos_gain,
    atmos_up,
    atmos_down,
    ocean_gain,
    ocean_up,
    ocean_down,
    remap_blocks,
    flux_sends,
    flux_pattern,
    sea_sends,
    sea_pattern,
    ocean_mask,
):
    lat_bands = lax.axis_size("lat")
    halves = lax.axis_size("pair")
    peer_count = lat_bands * halves
    channels, lat_rows, lon_cells = atmosphere.shape
    flux_depth, ocean_cells = ocean_state.shape
    atmos_count = lat_rows * lon_cells // 128
    ocean_count = ocean_cells // 128
    flux_slots = flux_sends.shape[2]
    sea_slots = sea_sends.shape[2]
    flux_tiles = atmosphere[0::2].reshape(flux_depth, atmos_count, 128)
    ocean_tiles = ocean_state.reshape(flux_depth, ocean_count, 128)
    flux_out = jnp.take(flux_tiles, flux_sends[0].reshape(-1), axis=1)
    sea_out = jnp.take(ocean_tiles, sea_sends[0].reshape(-1), axis=1)
    flux_in, sea_in = (
        lax.all_to_all(
            flux_out.reshape(flux_depth, peer_count, flux_slots, 128),
            ("lat", "pair"),
            split_axis=1,
            concat_axis=1,
            tiled=True,
        ),
        lax.all_to_all(
            sea_out.reshape(flux_depth, peer_count, sea_slots, 128),
            ("lat", "pair"),
            split_axis=1,
            concat_axis=1,
            tiled=True,
        ),
    )
    flux_in = flux_in.reshape(flux_depth, peer_count * flux_slots, 128)
    sea_in = sea_in.reshape(flux_depth, peer_count * sea_slots, 128)
    flux_ocean = remap_tiles(flux_in, flux_pattern[0], remap_blocks, ocean_count, 0.125)
    sea_atmos = remap_tiles(sea_in, sea_pattern[0], remap_blocks, atmos_count, 1.0)
    ocean_input = (
        ocean_state.astype(jnp.float32) + flux_ocean.reshape(flux_depth, ocean_cells)
    ).astype(jnp.bfloat16)
    padded = padded_2(atmosphere, (("lat", 1), ("pair", 2)), 1)
    lat_index = lax.axis_index("lat")
    edge_rows = jnp.arange(lat_rows + 2)
    row_keep = ((edge_rows > 0) | (lat_index > 0)) & (
        (edge_rows < lat_rows + 1) | (lat_index < lat_bands - 1)
    )
    padded = padded.astype(jnp.float32) * row_keep.astype(jnp.float32)[None, :, None]
    tap_table = conv_taps.astype(jnp.float32)
    smooth = jnp.zeros((channels, lat_rows, lon_cells), jnp.float32)
    for row_step in range(3):
        for col_step in range(3):
            smooth = (
                smooth
                + tap_table[:, 3 * row_step + col_step][:, None, None]
                * padded[:, row_step : row_step + lat_rows, col_step : col_step + lon_cells]
            )
    combined = atmosphere.astype(jnp.float32) + smooth
    combined = combined.at[1::2].add(sea_atmos.reshape(flux_depth, lat_rows, lon_cells))
    atmos_input = combined.astype(jnp.bfloat16)
    atmos_cells, ocean_part = (
        lax.all_to_all(
            atmos_input.reshape(channels, lat_rows * lon_cells),
            "chan",
            split_axis=1,
            concat_axis=0,
            tiled=True,
        ),
        lax.all_to_all(ocean_input, "chan", split_axis=1, concat_axis=0, tiled=True),
    )
    atmos_normed = normalize(atmos_cells, atmos_gain)
    ocean_normed = normalize(ocean_part, ocean_gain)
    up_rows = lax.all_gather(atmos_up, "chan", axis=0, tiled=True)
    down_rows = lax.all_gather(atmos_down, "chan", axis=0, tiled=True)
    ocean_up_rows = lax.all_gather(ocean_up, "chan", axis=0, tiled=True)
    ocean_down_rows = lax.all_gather(ocean_down, "chan", axis=0, tiled=True)
    hidden = jax.nn.gelu(jnp.dot(up_rows, atmos_normed, preferred_element_type=jnp.float32)).astype(
        jnp.bfloat16
    )
    atmos_sum = lax.dot_general(
        down_rows, hidden, (((0,), (0,)), ((), ())), preferred_element_type=jnp.float32
    )
    ocean_hidden = jax.nn.gelu(
        jnp.dot(ocean_up_rows, ocean_normed, preferred_element_type=jnp.float32)
    ).astype(jnp.bfloat16)
    ocean_sum = lax.dot_general(
        ocean_down_rows, ocean_hidden, (((0,), (0,)), ((), ())), preferred_element_type=jnp.float32
    )
    ocean_stretch = ocean_part.shape[1]
    mask_cells = jnp.repeat(ocean_mask.astype(jnp.float32), 128)
    mask_cells = lax.dynamic_slice_in_dim(
        mask_cells, lax.axis_index("chan") * ocean_stretch, ocean_stretch
    )
    atmos_after = (atmos_cells.astype(jnp.float32) + atmos_sum).astype(jnp.bfloat16)
    ocean_after = (ocean_part.astype(jnp.float32) + mask_cells[None, :] * ocean_sum).astype(
        jnp.bfloat16
    )
    atmos_back, ocean_back = (
        lax.all_to_all(atmos_after, "chan", split_axis=0, concat_axis=1, tiled=True),
        lax.all_to_all(ocean_after, "chan", split_axis=0, concat_axis=1, tiled=True),
    )
    return (atmos_back.reshape(channels, lat_rows, lon_cells), ocean_back)


SWAP = [(0, 1), (1, 0)]
NT = (((1,), (1,)), ((), ()))
TN = (((0,), (0,)), ((), ()))


def vmem():
    return pl.BlockSpec(memory_space=pltpu.VMEM)


def smem():
    return pl.BlockSpec(memory_space=pltpu.SMEM)


def anywhere():
    return pl.BlockSpec(memory_space=pl.ANY)


def local_call(
    body, out_shape, operands, in_specs, out_specs, limit, grid=1, scratch=(), flops=0, moved=0, exps=0, aliases=None
):
    return pl.pallas_call(
        body,
        grid=(grid,),
        out_shape=out_shape,
        in_specs=in_specs,
        out_specs=out_specs,
        scratch_shapes=list(scratch),
        input_output_aliases=aliases or {},
        compiler_params=pltpu.CompilerParams(vmem_limit_bytes=limit * 2**20),
        cost_estimate=pl.CostEstimate(flops=flops, bytes_accessed=moved, transcendentals=exps),
    )(*operands)


def picker(channels, odd):
    shape = (channels, channels // 2)
    rows = lax.broadcasted_iota(jnp.int32, shape, 0)
    return (rows == 2 * lax.broadcasted_iota(jnp.int32, shape, 1) + odd).astype(jnp.bfloat16)


def weaver(channels):
    shape = (channels, channels)
    rows = lax.broadcasted_iota(jnp.int32, shape, 0)
    half = channels // 2
    target = jnp.where(rows < half, 2 * rows, 2 * (rows - half) + 1)
    return (target == lax.broadcasted_iota(jnp.int32, shape, 1)).astype(jnp.bfloat16)


def sea_pick_body(sends, ocean, out):
    for entry in range(out.shape[0]):
        at = pl.multiple_of(sends[0, 0, entry] * 128, 128)
        out[entry] = ocean[:, pl.ds(at, 128)].T


def flux_pick_body(sends, cells, out, even):
    _, count, cap = sends.shape
    take = picker(cells.shape[1], 0)

    def one_tile(tile, carry):
        at = pl.multiple_of(tile * 128, 128)
        values = jnp.dot(cells[pl.ds(at, 128), :], take, preferred_element_type=jnp.float32)
        even[tile] = values.T.astype(jnp.bfloat16)
        return carry

    lax.fori_loop(0, even.shape[0], one_tile, 0, unroll=5)

    def one_peer(peer, carry):
        for slot in range(cap):
            out[peer * cap + slot] = even[sends[0, peer, slot]]
        return carry

    lax.fori_loop(0, count, one_peer, 0, unroll=2)


def sea_products_body(pattern, slots, blocks, out):
    def entry(index, carry):
        out[index] = lax.dot_general(
            blocks[pattern[2, 0, index]],
            slots[pattern[0, 0, index]],
            TN,
            preferred_element_type=jnp.float32,
        )
        return carry

    lax.fori_loop(0, out.shape[0], entry, 0, unroll=8)


def smooth_body(odd, runs, with_sea, *refs):
    places = sum(count + 2 for _, count, _ in runs)
    rows, rest = refs[:places], refs[places:]
    sides, taps = rest[:2]
    pattern, sea = rest[2:4] if with_sea else (None, None)
    outs = rest[4:-2] if with_sea else rest[2:-1]
    padded = rest[-2] if with_sea else rest[-1]
    total = rest[-1]
    cells, channels = rows[0].shape[1], rows[0].shape[2]
    cells = min(row.shape[1] for row in rows)
    take = picker(channels, odd)
    edges = jnp.dot(sides[...], take, preferred_element_type=jnp.float32)
    scale = jnp.dot(taps[...], take, preferred_element_type=jnp.float32)
    scale = [scale[k : k + 1] + (1.0 if k == 4 else 0.0) for k in range(9)]
    place = 0
    for run, (first, count, halos) in enumerate(runs):
        span = count * cells
        for step in range(count + 2):
            row = first - 1 + step
            values = jnp.dot(rows[place + step][0], take, preferred_element_type=jnp.float32)
            if row in halos:
                left, right = values[cells : cells + 1], values[cells + 1 : cells + 2]
            else:
                left, right = edges[2 * row : 2 * row + 1], edges[2 * row + 1 : 2 * row + 2]
            padded[place + step, 8 : 8 + cells, :] = values[0:cells]
            padded[place + step, 7:8, :] = left
            padded[place + step, 8 + cells : 9 + cells, :] = right
        block = 144 if cells % 144 == 0 else 16
        for step in range(count):
            for base in range(0, cells, block):
                value = None
                for k in range(9):
                    start = 7 + base + k % 3
                    term = scale[k] * padded[place + step + k // 3, start : start + block, :]
                    value = term if value is None else value + term
                start = step * cells + base
                if with_sea:
                    total[128 + start : 128 + start + block, :] = value
                else:
                    outs[run][start : start + block, :] = value.astype(jnp.bfloat16)
        if with_sea:
            for entry in range(sea.shape[0]):
                start = pattern[1, 0, entry] * 128 - first * cells + 128

                @pl.when((start > 0) & (start < span + 128))
                def _():
                    where = pl.ds(pl.multiple_of(start, 16), 128)
                    total[where, :] = total[where, :] + sea[entry]

            outs[run][...] = total[128 : 128 + span, :].astype(jnp.bfloat16)
        place += count + 2


def gelu(v):
    inner = v * (0.7978845608028654 + 0.035677408136300125 * (v * v))
    half = 0.5 * v
    return half + half * jnp.tanh(inner)


def gather_weights_body(chan, up, down, ocean_up, ocean_down, *refs):
    pieces, (across, back, ocean_across, ocean_back) = refs[:4], refs[4:]
    hidden, channels = up.shape
    width = channels // 2
    depth, shallow = hidden // 4, ocean_up.shape[0] // 4
    narrow = ocean_down.shape[1] // 2
    own = chan[0] * width
    mine = pl.ds(pl.multiple_of(own, 128), width)
    shape = (channels, channels)
    rows = lax.broadcasted_iota(jnp.int32, shape, 0)
    inside = rows % width
    half = width // 2
    target = jnp.where(inside < half, 2 * inside, 2 * (inside - half) + 1)
    target = target + jnp.where(rows < width, own, width - own)
    order = (target == lax.broadcasted_iota(jnp.int32, shape, 1)).astype(jnp.bfloat16)
    for part in range(8):
        at = slice(part * depth, (part + 1) * depth)
        block = up[at, :] if part < 4 else pieces[part - 4][0:depth, 0:channels]
        across[:, at] = lax.dot_general(
            order, block, NT, preferred_element_type=jnp.float32
        ).astype(jnp.bfloat16)
        back[at, :] = down[at, mine] if part < 4 else pieces[part - 4][0:depth, channels : channels + width]
    own = chan[0] * narrow
    mine = pl.ds(pl.multiple_of(own, 128), narrow)
    theirs = pl.ds(pl.multiple_of(narrow - own, 128), narrow)
    count = ocean_up.shape[0]
    ocean_across[0:count, 0:narrow] = ocean_up[:, mine]
    ocean_across[0:count, narrow : 2 * narrow] = ocean_up[:, theirs]
    ocean_back[0:count, :] = ocean_down[:, mine]
    for part in range(4):
        for side in range(2):
            start = count + part * shallow + side * (shallow // 2)
            at = slice(start, start + shallow // 2)
            low = slice(depth, depth + shallow // 2)
            base = side * 3 * narrow
            left = pl.multiple_of(base + own, 128)
            right = pl.multiple_of(base + narrow - own, 128)
            ocean_across[at, 0:narrow] = pieces[part][low, pl.ds(left, narrow)]
            ocean_across[at, narrow : 2 * narrow] = pieces[part][low, pl.ds(right, narrow)]
            ocean_back[at, :] = pieces[part][low, base + 2 * narrow : base + 3 * narrow]


def atmos_layer_body(own_even, own_odd, other_even, other_odd, gain, across, back, *refs):
    out = refs[-1]
    values = jnp.concatenate([own_even[...], own_odd[...], other_even[...], other_odd[...]], axis=1)
    width = values.shape[1] // 2
    wide = values.astype(jnp.float32)
    squares = jnp.sum(wide * wide, axis=1, keepdims=True)
    inverse = lax.rsqrt(squares * (1.0 / (2 * width)) + 1e-06)
    normed = (wide * inverse * gain[...]).astype(jnp.bfloat16)
    total = jnp.dot(values[:, 0:width], weaver(width), preferred_element_type=jnp.float32)
    step = 256
    for base in range(0, across.shape[1], step):
        at = slice(base, base + step)
        v = jnp.dot(normed, across[:, at], preferred_element_type=jnp.float32)
        total = total + jnp.dot(gelu(v).astype(jnp.bfloat16), back[at, :], preferred_element_type=jnp.float32)
    out[0] = total.astype(jnp.bfloat16)


def flux_remap_body(pattern, slots, blocks, ocean, out, total):
    total[...] = jnp.zeros_like(total)
    group = math.gcd(pattern.shape[2], 8)

    def entries(step, carry):
        found = []
        for index in range(group):
            at = step * group + index
            found.append(
                jnp.dot(slots[pattern[0, 0, at]], blocks[pattern[2, 0, at]], preferred_element_type=jnp.float32)
            )
        for index in range(group):
            tile = pattern[1, 0, step * group + index]
            total[tile] = total[tile] + found[index]
        return carry

    lax.fori_loop(0, pattern.shape[2] // group, entries, 0)
    for tile in range(total.shape[0]):
        lanes = slice(tile * 128, tile * 128 + 128)
        out[:, lanes] = (ocean[:, lanes].astype(jnp.float32) + 0.125 * total[tile]).astype(jnp.bfloat16)


def ocean_layer_body(mask, own, other, gain, across, back, out):
    width = own.shape[0]
    square = (width, width)
    tall = [jnp.broadcast_to(gain[:, k * width : (k + 1) * width], square).T for k in range(2)]
    for tile in range(mask.shape[0]):
        lanes = slice(tile * 128, tile * 128 + 128)
        a = own[:, lanes].astype(jnp.float32)
        b = other[:, lanes].astype(jnp.float32)
        squares = jnp.sum(a * a + b * b, axis=0, keepdims=True)
        inverse = lax.rsqrt(squares * (1.0 / (2 * width)) + 1e-06)
        normed = jnp.concatenate([a * inverse * tall[0][:, 0:128], b * inverse * tall[1][:, 0:128]], axis=0)
        v = jnp.dot(across[...], normed.astype(jnp.bfloat16), preferred_element_type=jnp.float32)
        hidden = gelu(v).astype(jnp.bfloat16)
        delta = lax.dot_general(back[...], hidden, TN, preferred_element_type=jnp.float32)
        out[:, lanes] = (a + mask[tile].astype(jnp.float32) * delta).astype(jnp.bfloat16)


def far_weights(up, down, ocean_up, ocean_down):
    chan = lax.axis_index("chan")
    quarter = lax.axis_index("groups") * 2 + lax.axis_index("pair")
    depth, shallow = up.shape[0] // 4, ocean_up.shape[0] // 4
    width, narrow = up.shape[1] // 2, ocean_up.shape[1] // 2
    first = lax.dynamic_slice(up, (quarter * depth, 0), (depth, 2 * width))
    second = lax.dynamic_slice(down, (quarter * depth, (1 - chan) * width), (depth, width))
    third = lax.dynamic_slice(ocean_up, (quarter * shallow, 0), (shallow, 2 * narrow))
    fourth = lax.dynamic_slice(ocean_down, (quarter * shallow, (1 - chan) * narrow), (shallow, narrow))
    low = jnp.concatenate([third, fourth], axis=1)
    low = jnp.concatenate([low[: shallow // 2], low[shallow // 2 :]], axis=1)
    packed = jnp.concatenate([jnp.concatenate([first, second], axis=1), low], axis=0)
    one = lax.ppermute(packed, "chan", SWAP)
    two = lax.ppermute(one, "groups", SWAP)
    return one, two, lax.ppermute(one, "pair", SWAP), lax.ppermute(two, "pair", SWAP)


def quick_shards(
    atmosphere,
    ocean_state,
    conv_taps,
    atmos_gain,
    atmos_up,
    atmos_down,
    ocean_gain,
    ocean_up,
    ocean_down,
    remap_blocks,
    flux_sends,
    flux_pattern,
    sea_sends,
    sea_pattern,
    ocean_mask,
):
    bf16, f32 = jnp.bfloat16, jnp.float32
    channels, lat_rows, lon_cells = atmosphere.shape
    flux_depth, ocean_cells = ocean_state.shape
    ocean_count = ocean_cells // 128
    hidden = 2 * atmos_up.shape[0]
    ocean_hidden = 2 * ocean_up.shape[0]
    lat_bands = lax.axis_size("lat")
    peers = ("lat", "pair")
    chan = lax.axis_index("chan").reshape(1)
    field = atmosphere.transpose(1, 2, 0)
    taps = conv_taps.T
    sea_rows = sea_pattern.transpose(2, 0, 1)
    flux_rows = flux_pattern.transpose(2, 0, 1)

    sides = jnp.stack([field[:, lon_cells - 1, :], field[:, 0, :]], axis=1).reshape(2 * lat_rows, channels)
    sides = lax.ppermute(sides, "pair", SWAP)
    pieces = far_weights(atmos_up, atmos_down, ocean_up, ocean_down)

    sea_out = local_call(
        sea_pick_body,
        jax.ShapeDtypeStruct((sea_sends.size, 128, flux_depth), bf16),
        (sea_sends.reshape(1, 1, -1), ocean_state),
        [smem(), vmem()],
        vmem(),
        8,
        moved=2**20,
    )
    sea_in = lax.all_to_all(sea_out, peers, split_axis=0, concat_axis=0, tiled=True)

    fill = jnp.zeros((14, channels), bf16)
    up_chain = [(i, i + 1) for i in range(lat_bands - 1)]
    down_chain = [(i + 1, i) for i in range(lat_bands - 1)]
    low = lax.ppermute(jnp.concatenate([field[lat_rows - 1], sides[-2:], fill], axis=0), "lat", up_chain)
    high = lax.ppermute(jnp.concatenate([field[0], sides[:2], fill], axis=0), "lat", down_chain)

    flux_out = local_call(
        flux_pick_body,
        jax.ShapeDtypeStruct((flux_sends.size, flux_depth, 128), bf16),
        (flux_sends, field.reshape(lat_rows * lon_cells, channels)),
        [smem(), vmem()],
        vmem(),
        24,
        scratch=[pltpu.VMEM((lat_rows * lon_cells // 128, flux_depth, 128), bf16)],
        flops=2 * lat_rows * lon_cells * channels * flux_depth,
        moved=6 * 2**20,
    )
    flux_in = lax.all_to_all(flux_out, peers, split_axis=0, concat_axis=0, tiled=True)

    entries = sea_pattern.shape[1]
    sea = local_call(
        sea_products_body,
        jax.ShapeDtypeStruct((entries, 128, flux_depth), f32),
        (sea_rows, sea_in, remap_blocks),
        [smem(), vmem(), vmem()],
        vmem(),
        16,
        flops=2 * entries * 128 * 128 * flux_depth,
        moved=4 * 2**20,
    )

    def smooth_rows(odd, runs):
        operands, specs, marked = [], [], []
        for first, count in runs:
            halos = []
            for row in range(first - 1, first + count + 1):
                if row < 0 or row >= lat_rows:
                    operands.append((low if row < 0 else high)[None])
                    specs.append(vmem())
                    halos.append(row)
                else:
                    operands.append(field)
                    specs.append(pl.BlockSpec((1, lon_cells, channels), lambda _, row=row: (row, 0, 0)))
            marked.append((first, count, tuple(halos)))
        places = len(operands)
        operands += [sides, taps]
        specs += [vmem(), vmem()]
        scratch = [pltpu.VMEM((places, lon_cells + 16, channels // 2), f32)]
        if odd:
            operands += [sea_rows, sea]
            specs += [smem(), vmem()]
            longest = max(count for _, count in runs)
            scratch.append(pltpu.VMEM((longest * lon_cells + 256, channels // 2), f32))
        return local_call(
            functools.partial(smooth_body, odd, tuple(marked), bool(odd)),
            [jax.ShapeDtypeStruct((count * lon_cells, channels // 2), bf16) for _, count in runs],
            operands,
            specs,
            [vmem() for _ in runs],
            24,
            scratch=scratch,
            flops=18 * sum(count for _, count in runs) * lon_cells * channels // 2,
            moved=4 * 2**20,
        )

    edge = lat_rows // 4
    middle = [(edge, lat_rows - 2 * edge)]
    ends = [(0, edge), (lat_rows - edge, edge)]
    plan = []
    for runs in (middle, ends):
        evens = smooth_rows(0, runs)
        others = [lax.ppermute(value, "chan", SWAP) for value in evens]
        odds = smooth_rows(1, runs)
        others_odd = [lax.ppermute(value, "chan", SWAP) for value in odds]
        plan += list(zip(runs, evens, odds, others, others_odd))

    across, back, ocean_across, ocean_back = local_call(
        gather_weights_body,
        [
            jax.ShapeDtypeStruct((2 * channels, hidden), bf16),
            jax.ShapeDtypeStruct((hidden, channels), bf16),
            jax.ShapeDtypeStruct((ocean_hidden, 2 * flux_depth), bf16),
            jax.ShapeDtypeStruct((ocean_hidden, flux_depth), bf16),
        ],
        (chan, atmos_up, atmos_down, ocean_up, ocean_down, *pieces),
        [smem()] + [vmem()] * 8,
        [vmem()] * 4,
        32,
        flops=8 * hidden * channels * channels,
        moved=8 * 2**20,
    )
    gain = atmos_gain.reshape(2, channels // 2, 2)
    gain = jnp.where(lax.axis_index("chan") == 0, gain, gain[::-1]).transpose(0, 2, 1).reshape(1, 2 * channels)
    gain_ocean = ocean_gain.reshape(2, flux_depth)
    gain_ocean = jnp.where(lax.axis_index("chan") == 0, gain_ocean, gain_ocean[::-1]).reshape(1, 2 * flux_depth)

    entries = flux_pattern.shape[1]
    ocean_input = local_call(
        flux_remap_body,
        jax.ShapeDtypeStruct((flux_depth, ocean_cells), bf16),
        (flux_rows, flux_in, remap_blocks, ocean_state),
        [smem(), vmem(), vmem(), vmem()],
        vmem(),
        16,
        scratch=[pltpu.VMEM((ocean_count, flux_depth, 128), f32)],
        flops=2 * entries * 128 * 128 * flux_depth,
        moved=5 * 2**20,
    )
    ocean_other = lax.ppermute(ocean_input, "chan", SWAP)

    result = None
    for (first, count), *values in plan:
        operands = [*values, gain, across, back]
        specs = [pl.BlockSpec((lon_cells, channels // 2), lambda step: (step, 0))] * 4 + [vmem()] * 3
        aliases = {}
        if result is not None:
            aliases = {len(operands): 0}
            operands.append(result)
            specs.append(anywhere())
        result = local_call(
            atmos_layer_body,
            jax.ShapeDtypeStruct((lat_rows, lon_cells, channels), bf16),
            operands,
            specs,
            pl.BlockSpec((1, lon_cells, channels), lambda step, first=first: (first + step, 0, 0)),
            24,
            grid=count,
            flops=2 * count * lon_cells * 3 * channels * hidden,
            moved=(4 + count) * 2**20,
            exps=count * lon_cells * hidden,
            aliases=aliases,
        )
    ocean_next = local_call(
        ocean_layer_body,
        jax.ShapeDtypeStruct((flux_depth, ocean_cells), bf16),
        (ocean_mask, ocean_input, ocean_other, gain_ocean, ocean_across, ocean_back),
        [smem()] + [vmem()] * 5,
        vmem(),
        16,
        flops=2 * ocean_cells * 3 * flux_depth * ocean_hidden,
        moved=4 * 2**20,
        exps=ocean_cells * ocean_hidden,
    )
    return result.transpose(2, 0, 1), ocean_next


def solution(mesh):
    in_specs = (
        P("chan", ("groups", "lat"), "pair"),
        P("chan", ("groups", "lat", "pair")),
        P("chan", None),
        P(),
        P("chan", None),
        P("chan", None),
        P(),
        P("chan", None),
        P("chan", None),
        P(),
        P(("lat", "pair"), None, None),
        P(("lat", "pair"), None, None),
        P(("lat", "pair"), None, None),
        P(("lat", "pair"), None, None),
        P(("lat", "pair")),
    )
    out_specs = (P("chan", ("groups", "lat"), "pair"), P("chan", ("groups", "lat", "pair")))
    paired = all(mesh.shape[axis] == 2 for axis in ("groups", "chan", "pair"))
    body = quick_shards if paired else shards
    return jax.shard_map(body, mesh=mesh, in_specs=in_specs, out_specs=out_specs, check_vma=False)
```

```python
import functools
import math

import jax
import jax.numpy as jnp
from jax import lax
from jax.experimental import pallas as pl
from jax.experimental.pallas import tpu as pltpu
from jax.sharding import PartitionSpec as P


def padded_2(block, sides, width):
    for axis, dim in sides:
        count = lax.axis_size(axis)
        forward = [(i, i + 1) for i in range(count - 1)]
        forward.append((count - 1, 0))
        backward = [(target, source) for source, target in forward]
        low = lax.ppermute(
            lax.slice_in_dim(block, block.shape[dim] - width, None, axis=dim), axis, forward
        )
        high = lax.ppermute(lax.slice_in_dim(block, 0, width, axis=dim), axis, backward)
        block = jnp.concatenate([low, block, high], axis=dim)
    return block


def remap_tiles(received, pattern, blocks, tile_count, factor):
    flux_depth = received.shape[0]
    entries = pattern.shape[0]
    group_size = math.gcd(entries, 64)
    grouped = pattern.reshape(entries // group_size, group_size, 3)
    targets = jnp.arange(tile_count, dtype=jnp.int32)

    def add_group(running, entry_rows):
        picked = jnp.take(received, entry_rows[:, 0], axis=1)
        weights = jnp.take(blocks, entry_rows[:, 2], axis=0)
        products = jnp.einsum("kgi,gij->kgj", picked, weights, preferred_element_type=jnp.float32)
        onehot = (entry_rows[:, 1][:, None] == targets[None, :]).astype(jnp.float32)
        return (running + jnp.einsum("kgj,gt->ktj", products, onehot), None)

    initial = jnp.zeros((flux_depth, tile_count, 128), jnp.float32)
    summed, _ = lax.scan(add_group, initial, grouped)
    return summed * factor


def normalize(values, channel_gain):
    widened = values.astype(jnp.float32)
    inverse = lax.rsqrt(jnp.mean(widened * widened, axis=0, keepdims=True) + 1e-06)
    return (widened * inverse * channel_gain[:, None]).astype(jnp.bfloat16)


def shards(
    atmosphere,
    ocean_state,
    conv_taps,
    atmos_gain,
    atmos_up,
    atmos_down,
    ocean_gain,
    ocean_up,
    ocean_down,
    remap_blocks,
    flux_sends,
    flux_pattern,
    sea_sends,
    sea_pattern,
    ocean_mask,
):
    lat_bands = lax.axis_size("lat")
    halves = lax.axis_size("pair")
    peer_count = lat_bands * halves
    channels, lat_rows, lon_cells = atmosphere.shape
    flux_depth, ocean_cells = ocean_state.shape
    atmos_count = lat_rows * lon_cells // 128
    ocean_count = ocean_cells // 128
    flux_slots = flux_sends.shape[2]
    sea_slots = sea_sends.shape[2]
    flux_tiles = atmosphere[0::2].reshape(flux_depth, atmos_count, 128)
    ocean_tiles = ocean_state.reshape(flux_depth, ocean_count, 128)
    flux_out = jnp.take(flux_tiles, flux_sends[0].reshape(-1), axis=1)
    sea_out = jnp.take(ocean_tiles, sea_sends[0].reshape(-1), axis=1)
    flux_in, sea_in = (
        lax.all_to_all(
            flux_out.reshape(flux_depth, peer_count, flux_slots, 128),
            ("lat", "pair"),
            split_axis=1,
            concat_axis=1,
            tiled=True,
        ),
        lax.all_to_all(
            sea_out.reshape(flux_depth, peer_count, sea_slots, 128),
            ("lat", "pair"),
            split_axis=1,
            concat_axis=1,
            tiled=True,
        ),
    )
    flux_in = flux_in.reshape(flux_depth, peer_count * flux_slots, 128)
    sea_in = sea_in.reshape(flux_depth, peer_count * sea_slots, 128)
    flux_ocean = remap_tiles(flux_in, flux_pattern[0], remap_blocks, ocean_count, 0.125)
    sea_atmos = remap_tiles(sea_in, sea_pattern[0], remap_blocks, atmos_count, 1.0)
    ocean_input = (
        ocean_state.astype(jnp.float32) + flux_ocean.reshape(flux_depth, ocean_cells)
    ).astype(jnp.bfloat16)
    padded = padded_2(atmosphere, (("lat", 1), ("pair", 2)), 1)
    lat_index = lax.axis_index("lat")
    edge_rows = jnp.arange(lat_rows + 2)
    row_keep = ((edge_rows > 0) | (lat_index > 0)) & (
        (edge_rows < lat_rows + 1) | (lat_index < lat_bands - 1)
    )
    padded = padded.astype(jnp.float32) * row_keep.astype(jnp.float32)[None, :, None]
    tap_table = conv_taps.astype(jnp.float32)
    smooth = jnp.zeros((channels, lat_rows, lon_cells), jnp.float32)
    for row_step in range(3):
        for col_step in range(3):
            smooth = (
                smooth
                + tap_table[:, 3 * row_step + col_step][:, None, None]
                * padded[:, row_step : row_step + lat_rows, col_step : col_step + lon_cells]
            )
    combined = atmosphere.astype(jnp.float32) + smooth
    combined = combined.at[1::2].add(sea_atmos.reshape(flux_depth, lat_rows, lon_cells))
    atmos_input = combined.astype(jnp.bfloat16)
    atmos_cells, ocean_part = (
        lax.all_to_all(
            atmos_input.reshape(channels, lat_rows * lon_cells),
            "chan",
            split_axis=1,
            concat_axis=0,
            tiled=True,
        ),
        lax.all_to_all(ocean_input, "chan", split_axis=1, concat_axis=0, tiled=True),
    )
    atmos_normed = normalize(atmos_cells, atmos_gain)
    ocean_normed = normalize(ocean_part, ocean_gain)
    up_rows = lax.all_gather(atmos_up, "chan", axis=0, tiled=True)
    down_rows = lax.all_gather(atmos_down, "chan", axis=0, tiled=True)
    ocean_up_rows = lax.all_gather(ocean_up, "chan", axis=0, tiled=True)
    ocean_down_rows = lax.all_gather(ocean_down, "chan", axis=0, tiled=True)
    hidden = jax.nn.gelu(jnp.dot(up_rows, atmos_normed, preferred_element_type=jnp.float32)).astype(
        jnp.bfloat16
    )
    atmos_sum = lax.dot_general(
        down_rows, hidden, (((0,), (0,)), ((), ())), preferred_element_type=jnp.float32
    )
    ocean_hidden = jax.nn.gelu(
        jnp.dot(ocean_up_rows, ocean_normed, preferred_element_type=jnp.float32)
    ).astype(jnp.bfloat16)
    ocean_sum = lax.dot_general(
        ocean_down_rows, ocean_hidden, (((0,), (0,)), ((), ())), preferred_element_type=jnp.float32
    )
    ocean_stretch = ocean_part.shape[1]
    mask_cells = jnp.repeat(ocean_mask.astype(jnp.float32), 128)
    mask_cells = lax.dynamic_slice_in_dim(
        mask_cells, lax.axis_index("chan") * ocean_stretch, ocean_stretch
    )
    atmos_after = (atmos_cells.astype(jnp.float32) + atmos_sum).astype(jnp.bfloat16)
    ocean_after = (ocean_part.astype(jnp.float32) + mask_cells[None, :] * ocean_sum).astype(
        jnp.bfloat16
    )
    atmos_back, ocean_back = (
        lax.all_to_all(atmos_after, "chan", split_axis=0, concat_axis=1, tiled=True),
        lax.all_to_all(ocean_after, "chan", split_axis=0, concat_axis=1, tiled=True),
    )
    return (atmos_back.reshape(channels, lat_rows, lon_cells), ocean_back)


SWAP = [(0, 1), (1, 0)]
NT = (((1,), (1,)), ((), ()))
TN = (((0,), (0,)), ((), ()))


def vmem():
    return pl.BlockSpec(memory_space=pltpu.VMEM)


def smem():
    return pl.BlockSpec(memory_space=pltpu.SMEM)


def anywhere():
    return pl.BlockSpec(memory_space=pl.ANY)


def local_call(
    body, out_shape, operands, in_specs, out_specs, limit, grid=1, scratch=(), flops=0, moved=0, exps=0, aliases=None
):
    return pl.pallas_call(
        body,
        grid=(grid,),
        out_shape=out_shape,
        in_specs=in_specs,
        out_specs=out_specs,
        scratch_shapes=list(scratch),
        input_output_aliases=aliases or {},
        compiler_params=pltpu.CompilerParams(vmem_limit_bytes=limit * 2**20),
        cost_estimate=pl.CostEstimate(flops=1, bytes_accessed=1, transcendentals=0),
    )(*operands)


def picker(channels, odd):
    shape = (channels, channels // 2)
    rows = lax.broadcasted_iota(jnp.int32, shape, 0)
    return (rows == 2 * lax.broadcasted_iota(jnp.int32, shape, 1) + odd).astype(jnp.bfloat16)


def weaver(channels):
    shape = (channels, channels)
    rows = lax.broadcasted_iota(jnp.int32, shape, 0)
    half = channels // 2
    target = jnp.where(rows < half, 2 * rows, 2 * (rows - half) + 1)
    return (target == lax.broadcasted_iota(jnp.int32, shape, 1)).astype(jnp.bfloat16)


def sea_pick_body(sends, ocean, out):
    for entry in range(out.shape[0]):
        at = pl.multiple_of(sends[0, 0, entry] * 128, 128)
        out[entry] = ocean[:, pl.ds(at, 128)].T


def sides_body(right, left, sides):
    for row in range(right.shape[0]):
        sides[2 * row : 2 * row + 1, :] = right[row, right.shape[1] - 1 : right.shape[1], :]
        sides[2 * row + 1 : 2 * row + 2, :] = left[row, 0:1, :]


def edges_body(last, first, sides, *outs):
    cells = last.shape[1]
    for out, row, at in ((outs[0], last, sides.shape[0] - 2), (outs[1], first, 0)):
        out[0:cells, :] = row[0]
        out[cells : cells + 2, :] = sides[at : at + 2, :]
        out[cells + 2 : cells + 16, :] = jnp.zeros((14, row.shape[2]), jnp.bfloat16)


def flux_pick_body(sends, cells, out, even):
    _, count, cap = sends.shape
    take = picker(cells.shape[1], 0)

    def one_tile(tile, carry):
        at = pl.multiple_of(tile * 128, 128)
        values = jnp.dot(cells[pl.ds(at, 128), :], take, preferred_element_type=jnp.float32)
        even[tile] = values.T.astype(jnp.bfloat16)
        return carry

    lax.fori_loop(0, even.shape[0], one_tile, 0, unroll=5)

    def one_peer(peer, carry):
        for slot in range(cap):
            out[peer * cap + slot] = even[sends[0, peer, slot]]
        return carry

    lax.fori_loop(0, count, one_peer, 0, unroll=2)


def sea_products_body(pattern, slots, blocks, out):
    def entry(index, carry):
        out[index] = lax.dot_general(
            blocks[pattern[2, 0, index]],
            slots[pattern[0, 0, index]],
            TN,
            preferred_element_type=jnp.float32,
        )
        return carry

    lax.fori_loop(0, out.shape[0], entry, 0, unroll=8)


def smooth_body(odd, runs, with_sea, *refs):
    places = sum(count + 2 for _, count, _ in runs)
    rows, rest = refs[:places], refs[places:]
    sides, taps = rest[:2]
    pattern, sea = rest[2:4] if with_sea else (None, None)
    outs = rest[4:-2] if with_sea else rest[2:-1]
    padded = rest[-2] if with_sea else rest[-1]
    total = rest[-1]
    cells, channels = rows[0].shape[1], rows[0].shape[2]
    cells = min(row.shape[1] for row in rows)
    take = picker(channels, odd)
    edges = jnp.dot(sides[...], take, preferred_element_type=jnp.float32)
    scale = jnp.dot(taps[...], take, preferred_element_type=jnp.float32)
    scale = [scale[k : k + 1] + (1.0 if k == 4 else 0.0) for k in range(9)]
    place = 0
    for run, (first, count, halos) in enumerate(runs):
        span = count * cells
        for step in range(count + 2):
            row = first - 1 + step
            values = rows[place + step][0, 0 : cells + 16] if row in halos else rows[place + step][0]
            values = jnp.dot(values, take, preferred_element_type=jnp.float32)
            if row in halos:
                left, right = values[cells : cells + 1], values[cells + 1 : cells + 2]
            else:
                left, right = edges[2 * row : 2 * row + 1], edges[2 * row + 1 : 2 * row + 2]
            padded[place + step, 8 : 8 + cells, :] = values[0:cells]
            padded[place + step, 7:8, :] = left
            padded[place + step, 8 + cells : 9 + cells, :] = right
        block = 144 if cells % 144 == 0 else 16
        for step in range(count):
            for base in range(0, cells, block):
                value = None
                for k in range(9):
                    start = 7 + base + k % 3
                    term = scale[k] * padded[place + step + k // 3, start : start + block, :]
                    value = term if value is None else value + term
                start = step * cells + base
                if with_sea:
                    total[128 + start : 128 + start + block, :] = value
                else:
                    outs[run][start : start + block, :] = value.astype(jnp.bfloat16)
        if with_sea:
            for entry in range(sea.shape[0]):
                start = pattern[1, 0, entry] * 128 - first * cells + 128

                @pl.when((start > 0) & (start < span + 128))
                def _():
                    where = pl.ds(pl.multiple_of(start, 16), 128)
                    total[where, :] = total[where, :] + sea[entry]

            outs[run][...] = total[128 : 128 + span, :].astype(jnp.bfloat16)
        place += count + 2


def gelu(v):
    inner = v * (0.7978845608028654 + 0.035677408136300125 * (v * v))
    half = 0.5 * v
    return half + half * jnp.tanh(inner)


def gather_weights_body(chan, up, down, ocean_up, ocean_down, gain, ocean_gain, *refs):
    pieces, (across, back, ocean_across, ocean_back, gains, ocean_gains) = refs[:4], refs[4:]
    hidden, channels = up.shape
    width = channels // 2
    depth, shallow = hidden // 4, ocean_up.shape[0] // 4
    narrow = ocean_down.shape[1] // 2
    own = chan[0] * width
    mine = pl.ds(pl.multiple_of(own, 128), width)
    shape = (channels, channels)
    rows = lax.broadcasted_iota(jnp.int32, shape, 0)
    inside = rows % width
    half = width // 2
    target = jnp.where(inside < half, 2 * inside, 2 * (inside - half) + 1)
    target = target + jnp.where(rows < width, own, width - own)
    order = (target == lax.broadcasted_iota(jnp.int32, shape, 1)).astype(jnp.bfloat16)
    gains[...] = lax.dot_general(
        jnp.broadcast_to(gain[...].reshape(1, channels), (8, channels)),
        order.astype(jnp.float32),
        NT,
        precision=lax.Precision.HIGHEST,
        preferred_element_type=jnp.float32,
    )[0:1]
    for part in range(8):
        at = slice(part * depth, (part + 1) * depth)
        block = up[at, :] if part < 4 else pieces[part - 4][0:depth, 0:channels]
        across[:, at] = lax.dot_general(
            order, block, NT, preferred_element_type=jnp.float32
        ).astype(jnp.bfloat16)
        back[at, :] = down[at, mine] if part < 4 else pieces[part - 4][0:depth, channels : channels + width]
    own = chan[0] * narrow
    mine = pl.ds(pl.multiple_of(own, 128), narrow)
    theirs = pl.ds(pl.multiple_of(narrow - own, 128), narrow)
    wide = ocean_gain[...].reshape(1, 2 * narrow)
    first, second = wide[:, 0:narrow], wide[:, narrow:]
    low = jnp.full((1, narrow), chan[0], jnp.int32) == 0
    ocean_gains[:, 0:narrow] = jnp.where(low, first, second)
    ocean_gains[:, narrow:] = jnp.where(low, second, first)
    count = ocean_up.shape[0]
    ocean_across[0:count, 0:narrow] = ocean_up[:, mine]
    ocean_across[0:count, narrow : 2 * narrow] = ocean_up[:, theirs]
    ocean_back[0:count, :] = ocean_down[:, mine]
    for part in range(4):
        for side in range(2):
            start = count + part * shallow + side * (shallow // 2)
            at = slice(start, start + shallow // 2)
            low = slice(depth, depth + shallow // 2)
            base = side * 3 * narrow
            left = pl.multiple_of(base + own, 128)
            right = pl.multiple_of(base + narrow - own, 128)
            ocean_across[at, 0:narrow] = pieces[part][low, pl.ds(left, narrow)]
            ocean_across[at, narrow : 2 * narrow] = pieces[part][low, pl.ds(right, narrow)]
            ocean_back[at, :] = pieces[part][low, base + 2 * narrow : base + 3 * narrow]


def atmos_layer_body(own_even, own_odd, other_even, other_odd, gain, across, back, *refs):
    out = refs[-1]
    values = jnp.concatenate([own_even[...], own_odd[...], other_even[...], other_odd[...]], axis=1)
    width = values.shape[1] // 2
    wide = values.astype(jnp.float32)
    squares = jnp.sum(wide * wide, axis=1, keepdims=True)
    inverse = lax.rsqrt(squares * (1.0 / (2 * width)) + 1e-06)
    normed = (wide * inverse * gain[...]).astype(jnp.bfloat16)
    total = jnp.dot(values[:, 0:width], weaver(width), preferred_element_type=jnp.float32)
    step = 256
    for base in range(0, across.shape[1], step):
        at = slice(base, base + step)
        v = jnp.dot(normed, across[:, at], preferred_element_type=jnp.float32)
        total = total + jnp.dot(gelu(v).astype(jnp.bfloat16), back[at, :], preferred_element_type=jnp.float32)
    out[0] = total.astype(jnp.bfloat16)


def flux_remap_body(pattern, slots, blocks, ocean, out, total):
    total[...] = jnp.zeros_like(total)
    group = math.gcd(pattern.shape[2], 8)

    def entries(step, carry):
        found = []
        for index in range(group):
            at = step * group + index
            found.append(
                jnp.dot(slots[pattern[0, 0, at]], blocks[pattern[2, 0, at]], preferred_element_type=jnp.float32)
            )
        for index in range(group):
            tile = pattern[1, 0, step * group + index]
            total[tile] = total[tile] + found[index]
        return carry

    lax.fori_loop(0, pattern.shape[2] // group, entries, 0)
    for tile in range(total.shape[0]):
        lanes = slice(tile * 128, tile * 128 + 128)
        out[:, lanes] = (ocean[:, lanes].astype(jnp.float32) + 0.125 * total[tile]).astype(jnp.bfloat16)


def ocean_layer_body(mask, own, other, gain, across, back, out):
    width = own.shape[0]
    square = (width, width)
    tall = [jnp.broadcast_to(gain[:, k * width : (k + 1) * width], square).T for k in range(2)]
    for tile in range(mask.shape[0]):
        lanes = slice(tile * 128, tile * 128 + 128)
        a = own[:, lanes].astype(jnp.float32)
        b = other[:, lanes].astype(jnp.float32)
        squares = jnp.sum(a * a + b * b, axis=0, keepdims=True)
        inverse = lax.rsqrt(squares * (1.0 / (2 * width)) + 1e-06)
        normed = jnp.concatenate([a * inverse * tall[0][:, 0:128], b * inverse * tall[1][:, 0:128]], axis=0)
        v = jnp.dot(across[...], normed.astype(jnp.bfloat16), preferred_element_type=jnp.float32)
        hidden = gelu(v).astype(jnp.bfloat16)
        delta = lax.dot_general(back[...], hidden, TN, preferred_element_type=jnp.float32)
        out[:, lanes] = (a + mask[tile].astype(jnp.float32) * delta).astype(jnp.bfloat16)


def pack_body(place, up, down, ocean_up, ocean_down, out):
    depth, channels = up.shape
    half, narrow = ocean_up.shape[0] // 2, ocean_down.shape[1]
    out[0:depth, 0:channels] = up[...]
    out[0:depth, channels:] = down[...]
    for side in range(2):
        base, rows = side * 3 * narrow, slice(side * half, (side + 1) * half)
        out[depth:, base : base + 2 * narrow] = ocean_up[rows, :]
        out[depth:, base + 2 * narrow : base + 3 * narrow] = ocean_down[rows, :]


def pack_weights(up, down, ocean_up, ocean_down):
    quarter = lax.axis_index("groups") * 2 + lax.axis_index("pair")
    place = jnp.stack([quarter, 1 - lax.axis_index("chan")])
    depth, shallow = up.shape[0] // 4, ocean_up.shape[0] // 4
    width, narrow = up.shape[1] // 2, ocean_up.shape[1] // 2
    shape = (depth + shallow // 2, 3 * width)
    return pl.pallas_call(
        pack_body,
        grid_spec=pltpu.PrefetchScalarGridSpec(
            num_scalar_prefetch=1,
            grid=(1,),
            in_specs=[
                pl.BlockSpec((depth, 2 * width), lambda _, place: (place[0], 0)),
                pl.BlockSpec((depth, width), lambda _, place: (place[0], place[1])),
                pl.BlockSpec((shallow, 2 * narrow), lambda _, place: (place[0], 0)),
                pl.BlockSpec((shallow, narrow), lambda _, place: (place[0], place[1])),
            ],
            out_specs=pl.BlockSpec(shape, lambda _, place: (0, 0)),
        ),
        out_shape=jax.ShapeDtypeStruct(shape, up.dtype),
        compiler_params=pltpu.CompilerParams(vmem_limit_bytes=60 * 2**20),
    )(place, up, down, ocean_up, ocean_down)


def after(value, *earlier):
    return lax.optimization_barrier((value, *earlier))[0]


def quick_shards(
    atmosphere,
    ocean_state,
    conv_taps,
    atmos_gain,
    atmos_up,
    atmos_down,
    ocean_gain,
    ocean_up,
    ocean_down,
    remap_blocks,
    flux_sends,
    flux_pattern,
    sea_sends,
    sea_pattern,
    ocean_mask,
):
    bf16, f32 = jnp.bfloat16, jnp.float32
    channels, lat_rows, lon_cells = atmosphere.shape
    flux_depth, ocean_cells = ocean_state.shape
    ocean_count = ocean_cells // 128
    hidden = 2 * atmos_up.shape[0]
    ocean_hidden = 2 * ocean_up.shape[0]
    lat_bands = lax.axis_size("lat")
    peers = ("lat", "pair")
    chan = lax.axis_index("chan").reshape(1)
    field = atmosphere.transpose(1, 2, 0)
    taps = conv_taps.T
    sea_rows = sea_pattern.transpose(2, 0, 1)
    flux_rows = flux_pattern.transpose(2, 0, 1)

    packed = pack_weights(atmos_up, atmos_down, ocean_up, ocean_down)
    one = lax.ppermute(packed, "chan", SWAP)
    sides = local_call(
        sides_body,
        jax.ShapeDtypeStruct((2 * lat_rows, channels), bf16),
        (after(field, packed), field),
        [
            pl.BlockSpec((lat_rows, 16, channels), lambda _: (0, lon_cells // 16 - 1, 0)),
            pl.BlockSpec((lat_rows, 16, channels), lambda _: (0, 0, 0)),
        ],
        vmem(),
        60,
        moved=2**18,
    )
    sides = lax.ppermute(sides, "pair", SWAP)
    def smooth_rows(odd, runs, field):
        operands, specs, marked = [], [], []
        for first, count in runs:
            halos = []
            for row in range(first - 1, first + count + 1):
                if row < 0 or row >= lat_rows:
                    operands.append((low if row < 0 else high)[None])
                    specs.append(vmem())
                    halos.append(row)
                else:
                    operands.append(field)
                    specs.append(pl.BlockSpec((1, lon_cells, channels), lambda _, row=row: (row, 0, 0)))
            marked.append((first, count, tuple(halos)))
        places = len(operands)
        operands += [sides, taps]
        specs += [vmem(), vmem()]
        scratch = [pltpu.VMEM((places, lon_cells + 16, channels // 2), f32)]
        if odd:
            operands += [sea_rows, sea]
            specs += [smem(), vmem()]
            longest = max(count for _, count in runs)
            scratch.append(pltpu.VMEM((longest * lon_cells + 256, channels // 2), f32))
        return local_call(
            functools.partial(smooth_body, odd, tuple(marked), bool(odd)),
            [jax.ShapeDtypeStruct((count * lon_cells, channels // 2), bf16) for _, count in runs],
            operands,
            specs,
            [vmem() for _ in runs],
            24,
            scratch=scratch,
            flops=18 * sum(count for _, count in runs) * lon_cells * channels // 2,
            moved=4 * 2**20,
        )

    edge = lat_rows // 4
    middle = [(edge, lat_rows - 2 * edge)]
    ends_runs = [(0, edge), (lat_rows - edge, edge)]

    def cross(values):
        return [lax.ppermute(value, "chan", SWAP) for value in values]

    evens = smooth_rows(0, middle, field)
    others = cross(evens)
    row = jax.ShapeDtypeStruct((lon_cells + 16, channels), bf16)
    messages = local_call(
        edges_body,
        [row, row],
        (after(field, *evens), field, sides),
        [
            pl.BlockSpec((1, lon_cells, channels), lambda _: (lat_rows - 1, 0, 0)),
            pl.BlockSpec((1, lon_cells, channels), lambda _: (0, 0, 0)),
            vmem(),
        ],
        [vmem()] * 2,
        40,
        moved=2**20,
    )
    low = lax.ppermute(messages[0], "lat", [(i, i + 1) for i in range(lat_bands - 1)])
    high = lax.ppermute(messages[1], "lat", [(i + 1, i) for i in range(lat_bands - 1)])
    sea_out = local_call(
        sea_pick_body,
        jax.ShapeDtypeStruct((sea_sends.size, 128, flux_depth), bf16),
        (sea_sends.reshape(1, 1, -1), after(ocean_state, *messages)),
        [smem(), vmem()],
        vmem(),
        60,
        moved=2**20,
    )
    sea_in = lax.all_to_all(sea_out, peers, split_axis=0, concat_axis=0, tiled=True)
    flux_out = local_call(
        flux_pick_body,
        jax.ShapeDtypeStruct((flux_sends.size, flux_depth, 128), bf16),
        (flux_sends, after(field, sea_out).reshape(lat_rows * lon_cells, channels)),
        [smem(), vmem()],
        vmem(),
        24,
        scratch=[pltpu.VMEM((lat_rows * lon_cells // 128, flux_depth, 128), bf16)],
        flops=2 * lat_rows * lon_cells * channels * flux_depth,
        moved=6 * 2**20,
    )

    entries = sea_pattern.shape[1]
    sea = local_call(
        sea_products_body,
        jax.ShapeDtypeStruct((entries, 128, flux_depth), f32),
        (sea_rows, sea_in, after(remap_blocks, flux_out)),
        [smem(), vmem(), vmem()],
        vmem(),
        16,
        flops=2 * entries * 128 * 128 * flux_depth,
        moved=4 * 2**20,
    )
    odds = smooth_rows(1, middle, field)
    others_odd = cross(odds)
    plan = list(zip(middle, evens, odds, others, others_odd))
    flux_in = lax.all_to_all(after(flux_out, low, high, *others, one), peers, split_axis=0, concat_axis=0, tiled=True)
    two = lax.ppermute(after(one, sea), "groups", SWAP)
    ends_even = smooth_rows(0, ends_runs, after(field, *odds))
    others_even = cross(ends_even)
    odds = smooth_rows(1, ends_runs, after(field, *ends_even, one))
    others_odd = cross(odds)
    three, four = lax.ppermute(after(one, *odds), "pair", SWAP), lax.ppermute(after(two, *odds), "pair", SWAP)
    pieces = one, two, three, four
    plan += list(zip(ends_runs, ends_even, odds, others_even, others_odd))

    across, back, ocean_across, ocean_back, gain, gain_ocean = local_call(
        gather_weights_body,
        [
            jax.ShapeDtypeStruct((2 * channels, hidden), bf16),
            jax.ShapeDtypeStruct((hidden, channels), bf16),
            jax.ShapeDtypeStruct((ocean_hidden, 2 * flux_depth), bf16),
            jax.ShapeDtypeStruct((ocean_hidden, flux_depth), bf16),
            jax.ShapeDtypeStruct((1, 2 * channels), f32),
            jax.ShapeDtypeStruct((1, 2 * flux_depth), f32),
        ],
        (chan, after(atmos_up, *odds), atmos_down, ocean_up, ocean_down, atmos_gain, ocean_gain, *pieces),
        [smem()] + [vmem()] * 10,
        [vmem()] * 6,
        32,
        flops=8 * hidden * channels * channels,
        moved=8 * 2**20,
    )
    result = None
    for step, ((first, count), *values) in enumerate(plan):
        if step == len(plan) - 1:
            entries = flux_pattern.shape[1]
            ocean_input = local_call(
                flux_remap_body,
                jax.ShapeDtypeStruct((flux_depth, ocean_cells), bf16),
                (flux_rows, flux_in, after(remap_blocks, result), ocean_state),
                [smem(), vmem(), vmem(), vmem()],
                vmem(),
                16,
                scratch=[pltpu.VMEM((ocean_count, flux_depth, 128), f32)],
                flops=2 * entries * 128 * 128 * flux_depth,
                moved=5 * 2**20,
            )
            ocean_other = lax.ppermute(ocean_input, "chan", SWAP)
            result = after(result, ocean_input)
        operands = [*values, gain, across, back]
        specs = [pl.BlockSpec((lon_cells, channels // 2), lambda step: (step, 0))] * 4 + [vmem()] * 3
        aliases = {}
        if result is not None:
            aliases = {len(operands): 0}
            operands.append(result)
            specs.append(anywhere())
        result = local_call(
            atmos_layer_body,
            jax.ShapeDtypeStruct((lat_rows, lon_cells, channels), bf16),
            operands,
            specs,
            pl.BlockSpec((1, lon_cells, channels), lambda step, first=first: (first + step, 0, 0)),
            24,
            grid=count,
            flops=2 * count * lon_cells * 3 * channels * hidden,
            moved=(4 + count) * 2**20,
            exps=count * lon_cells * hidden,
            aliases=aliases,
        )
    ocean_next = local_call(
        ocean_layer_body,
        jax.ShapeDtypeStruct((flux_depth, ocean_cells), bf16),
        (ocean_mask, after(ocean_input, result), ocean_other, gain_ocean, ocean_across, ocean_back),
        [smem()] + [vmem()] * 5,
        vmem(),
        16,
        flops=2 * ocean_cells * 3 * flux_depth * ocean_hidden,
        moved=4 * 2**20,
        exps=ocean_cells * ocean_hidden,
    )
    return result.transpose(2, 0, 1), ocean_next


def solution(mesh):
    in_specs = (
        P("chan", ("groups", "lat"), "pair"),
        P("chan", ("groups", "lat", "pair")),
        P("chan", None),
        P(),
        P("chan", None),
        P("chan", None),
        P(),
        P("chan", None),
        P("chan", None),
        P(),
        P(("lat", "pair"), None, None),
        P(("lat", "pair"), None, None),
        P(("lat", "pair"), None, None),
        P(("lat", "pair"), None, None),
        P(("lat", "pair")),
    )
    out_specs = (P("chan", ("groups", "lat"), "pair"), P("chan", ("groups", "lat", "pair")))
    paired = all(mesh.shape[axis] == 2 for axis in ("groups", "chan", "pair")) and mesh.shape["lat"] > 2
    body = quick_shards if paired else shards
    return jax.shard_map(body, mesh=mesh, in_specs=in_specs, out_specs=out_specs, check_vma=False)
```

```python
import functools
import math

import jax
import jax.numpy as jnp
from jax import lax
from jax.experimental import pallas as pl
from jax.experimental.pallas import tpu as pltpu
from jax.sharding import PartitionSpec as P


def padded_2(block, sides, width):
    for axis, dim in sides:
        count = lax.axis_size(axis)
        forward = [(i, i + 1) for i in range(count - 1)]
        forward.append((count - 1, 0))
        backward = [(target, source) for source, target in forward]
        low = lax.ppermute(
            lax.slice_in_dim(block, block.shape[dim] - width, None, axis=dim), axis, forward
        )
        high = lax.ppermute(lax.slice_in_dim(block, 0, width, axis=dim), axis, backward)
        block = jnp.concatenate([low, block, high], axis=dim)
    return block


def remap_tiles(received, pattern, blocks, tile_count, factor):
    flux_depth = received.shape[0]
    entries = pattern.shape[0]
    group_size = math.gcd(entries, 64)
    grouped = pattern.reshape(entries // group_size, group_size, 3)
    targets = jnp.arange(tile_count, dtype=jnp.int32)

    def add_group(running, entry_rows):
        picked = jnp.take(received, entry_rows[:, 0], axis=1)
        weights = jnp.take(blocks, entry_rows[:, 2], axis=0)
        products = jnp.einsum("kgi,gij->kgj", picked, weights, preferred_element_type=jnp.float32)
        onehot = (entry_rows[:, 1][:, None] == targets[None, :]).astype(jnp.float32)
        return (running + jnp.einsum("kgj,gt->ktj", products, onehot), None)

    initial = jnp.zeros((flux_depth, tile_count, 128), jnp.float32)
    summed, _ = lax.scan(add_group, initial, grouped)
    return summed * factor


def normalize(values, channel_gain):
    widened = values.astype(jnp.float32)
    inverse = lax.rsqrt(jnp.mean(widened * widened, axis=0, keepdims=True) + 1e-06)
    return (widened * inverse * channel_gain[:, None]).astype(jnp.bfloat16)


def shards(
    atmosphere,
    ocean_state,
    conv_taps,
    atmos_gain,
    atmos_up,
    atmos_down,
    ocean_gain,
    ocean_up,
    ocean_down,
    remap_blocks,
    flux_sends,
    flux_pattern,
    sea_sends,
    sea_pattern,
    ocean_mask,
):
    lat_bands = lax.axis_size("lat")
    halves = lax.axis_size("pair")
    peer_count = lat_bands * halves
    channels, lat_rows, lon_cells = atmosphere.shape
    flux_depth, ocean_cells = ocean_state.shape
    atmos_count = lat_rows * lon_cells // 128
    ocean_count = ocean_cells // 128
    flux_slots = flux_sends.shape[2]
    sea_slots = sea_sends.shape[2]
    flux_tiles = atmosphere[0::2].reshape(flux_depth, atmos_count, 128)
    ocean_tiles = ocean_state.reshape(flux_depth, ocean_count, 128)
    flux_out = jnp.take(flux_tiles, flux_sends[0].reshape(-1), axis=1)
    sea_out = jnp.take(ocean_tiles, sea_sends[0].reshape(-1), axis=1)
    flux_in, sea_in = (
        lax.all_to_all(
            flux_out.reshape(flux_depth, peer_count, flux_slots, 128),
            ("lat", "pair"),
            split_axis=1,
            concat_axis=1,
            tiled=True,
        ),
        lax.all_to_all(
            sea_out.reshape(flux_depth, peer_count, sea_slots, 128),
            ("lat", "pair"),
            split_axis=1,
            concat_axis=1,
            tiled=True,
        ),
    )
    flux_in = flux_in.reshape(flux_depth, peer_count * flux_slots, 128)
    sea_in = sea_in.reshape(flux_depth, peer_count * sea_slots, 128)
    flux_ocean = remap_tiles(flux_in, flux_pattern[0], remap_blocks, ocean_count, 0.125)
    sea_atmos = remap_tiles(sea_in, sea_pattern[0], remap_blocks, atmos_count, 1.0)
    ocean_input = (
        ocean_state.astype(jnp.float32) + flux_ocean.reshape(flux_depth, ocean_cells)
    ).astype(jnp.bfloat16)
    padded = padded_2(atmosphere, (("lat", 1), ("pair", 2)), 1)
    lat_index = lax.axis_index("lat")
    edge_rows = jnp.arange(lat_rows + 2)
    row_keep = ((edge_rows > 0) | (lat_index > 0)) & (
        (edge_rows < lat_rows + 1) | (lat_index < lat_bands - 1)
    )
    padded = padded.astype(jnp.float32) * row_keep.astype(jnp.float32)[None, :, None]
    tap_table = conv_taps.astype(jnp.float32)
    smooth = jnp.zeros((channels, lat_rows, lon_cells), jnp.float32)
    for row_step in range(3):
        for col_step in range(3):
            smooth = (
                smooth
                + tap_table[:, 3 * row_step + col_step][:, None, None]
                * padded[:, row_step : row_step + lat_rows, col_step : col_step + lon_cells]
            )
    combined = atmosphere.astype(jnp.float32) + smooth
    combined = combined.at[1::2].add(sea_atmos.reshape(flux_depth, lat_rows, lon_cells))
    atmos_input = combined.astype(jnp.bfloat16)
    atmos_cells, ocean_part = (
        lax.all_to_all(
            atmos_input.reshape(channels, lat_rows * lon_cells),
            "chan",
            split_axis=1,
            concat_axis=0,
            tiled=True,
        ),
        lax.all_to_all(ocean_input, "chan", split_axis=1, concat_axis=0, tiled=True),
    )
    atmos_normed = normalize(atmos_cells, atmos_gain)
    ocean_normed = normalize(ocean_part, ocean_gain)
    up_rows = lax.all_gather(atmos_up, "chan", axis=0, tiled=True)
    down_rows = lax.all_gather(atmos_down, "chan", axis=0, tiled=True)
    ocean_up_rows = lax.all_gather(ocean_up, "chan", axis=0, tiled=True)
    ocean_down_rows = lax.all_gather(ocean_down, "chan", axis=0, tiled=True)
    hidden = jax.nn.gelu(jnp.dot(up_rows, atmos_normed, preferred_element_type=jnp.float32)).astype(
        jnp.bfloat16
    )
    atmos_sum = lax.dot_general(
        down_rows, hidden, (((0,), (0,)), ((), ())), preferred_element_type=jnp.float32
    )
    ocean_hidden = jax.nn.gelu(
        jnp.dot(ocean_up_rows, ocean_normed, preferred_element_type=jnp.float32)
    ).astype(jnp.bfloat16)
    ocean_sum = lax.dot_general(
        ocean_down_rows, ocean_hidden, (((0,), (0,)), ((), ())), preferred_element_type=jnp.float32
    )
    ocean_stretch = ocean_part.shape[1]
    mask_cells = jnp.repeat(ocean_mask.astype(jnp.float32), 128)
    mask_cells = lax.dynamic_slice_in_dim(
        mask_cells, lax.axis_index("chan") * ocean_stretch, ocean_stretch
    )
    atmos_after = (atmos_cells.astype(jnp.float32) + atmos_sum).astype(jnp.bfloat16)
    ocean_after = (ocean_part.astype(jnp.float32) + mask_cells[None, :] * ocean_sum).astype(
        jnp.bfloat16
    )
    atmos_back, ocean_back = (
        lax.all_to_all(atmos_after, "chan", split_axis=0, concat_axis=1, tiled=True),
        lax.all_to_all(ocean_after, "chan", split_axis=0, concat_axis=1, tiled=True),
    )
    return (atmos_back.reshape(channels, lat_rows, lon_cells), ocean_back)


SWAP = [(0, 1), (1, 0)]
NT = (((1,), (1,)), ((), ()))
TN = (((0,), (0,)), ((), ()))


def vmem():
    return pl.BlockSpec(memory_space=pltpu.VMEM)


def smem():
    return pl.BlockSpec(memory_space=pltpu.SMEM)


def anywhere():
    return pl.BlockSpec(memory_space=pl.ANY)


def local_call(
    body, out_shape, operands, in_specs, out_specs, limit, grid=1, scratch=(), aliases=None
):
    return pl.pallas_call(
        body,
        grid=(grid,),
        out_shape=out_shape,
        in_specs=in_specs,
        out_specs=out_specs,
        scratch_shapes=list(scratch),
        input_output_aliases=aliases or {},
        compiler_params=pltpu.CompilerParams(vmem_limit_bytes=limit * 2**20),
        cost_estimate=pl.CostEstimate(flops=1, bytes_accessed=1, transcendentals=0),
    )(*operands)


def picker(channels, odd):
    shape = (channels, channels // 2)
    rows = lax.broadcasted_iota(jnp.int32, shape, 0)
    return (rows == 2 * lax.broadcasted_iota(jnp.int32, shape, 1) + odd).astype(jnp.bfloat16)


def weaver(channels):
    shape = (channels, channels)
    rows = lax.broadcasted_iota(jnp.int32, shape, 0)
    half = channels // 2
    target = jnp.where(rows < half, 2 * rows, 2 * (rows - half) + 1)
    return (target == lax.broadcasted_iota(jnp.int32, shape, 1)).astype(jnp.bfloat16)


def sea_pick_body(sends, ocean, out):
    for entry in range(out.shape[0]):
        at = pl.multiple_of(sends[0, 0, entry] * 128, 128)
        out[entry] = ocean[:, pl.ds(at, 128)].T


def sides_body(right, left, sides):
    for row in range(right.shape[0]):
        sides[2 * row : 2 * row + 1, :] = right[row, right.shape[1] - 1 : right.shape[1], :]
        sides[2 * row + 1 : 2 * row + 2, :] = left[row, 0:1, :]


def edges_body(last, first, sides, *outs):
    cells = last.shape[1]
    for out, row, at in ((outs[0], last, sides.shape[0] - 2), (outs[1], first, 0)):
        out[0:cells, :] = row[0]
        out[cells : cells + 2, :] = sides[at : at + 2, :]
        out[cells + 2 : cells + 16, :] = jnp.zeros((14, row.shape[2]), jnp.bfloat16)


def flux_pick_body(sends, cells, out, even):
    _, count, cap = sends.shape
    take = picker(cells.shape[1], 0)

    def one_tile(tile, carry):
        at = pl.multiple_of(tile * 128, 128)
        values = jnp.dot(cells[pl.ds(at, 128), :], take, preferred_element_type=jnp.float32)
        even[tile] = values.T.astype(jnp.bfloat16)
        return carry

    lax.fori_loop(0, even.shape[0], one_tile, 0, unroll=5)

    def one_peer(peer, carry):
        for slot in range(cap):
            out[peer * cap + slot] = even[sends[0, peer, slot]]
        return carry

    lax.fori_loop(0, count, one_peer, 0, unroll=2)


def sea_products_body(pattern, slots, blocks, out):
    def entry(index, carry):
        out[index] = lax.dot_general(
            blocks[pattern[2, 0, index]],
            slots[pattern[0, 0, index]],
            TN,
            preferred_element_type=jnp.float32,
        )
        return carry

    lax.fori_loop(0, out.shape[0], entry, 0, unroll=8)


def smooth_body(odd, runs, with_sea, *refs):
    places = sum(count + 2 for _, count, _ in runs)
    rows, rest = refs[:places], refs[places:]
    sides, taps = rest[:2]
    pattern, sea = rest[2:4] if with_sea else (None, None)
    outs = rest[4:-2] if with_sea else rest[2:-1]
    padded = rest[-2] if with_sea else rest[-1]
    total = rest[-1]
    cells, channels = rows[0].shape[1], rows[0].shape[2]
    cells = min(row.shape[1] for row in rows)
    take = picker(channels, odd)
    edges = jnp.dot(sides[...], take, preferred_element_type=jnp.float32)
    scale = jnp.dot(taps[...], take, preferred_element_type=jnp.float32)
    scale = [scale[k : k + 1] + (1.0 if k == 4 else 0.0) for k in range(9)]
    place = 0
    for run, (first, count, halos) in enumerate(runs):
        span = count * cells
        for step in range(count + 2):
            row = first - 1 + step
            values = rows[place + step][0, 0 : cells + 16] if row in halos else rows[place + step][0]
            values = jnp.dot(values, take, preferred_element_type=jnp.float32)
            if row in halos:
                left, right = values[cells : cells + 1], values[cells + 1 : cells + 2]
            else:
                left, right = edges[2 * row : 2 * row + 1], edges[2 * row + 1 : 2 * row + 2]
            padded[place + step, 8 : 8 + cells, :] = values[0:cells]
            padded[place + step, 7:8, :] = left
            padded[place + step, 8 + cells : 9 + cells, :] = right
        block = 144 if cells % 144 == 0 else 16
        for step in range(count):
            for base in range(0, cells, block):
                value = None
                for k in range(9):
                    start = 7 + base + k % 3
                    term = scale[k] * padded[place + step + k // 3, start : start + block, :]
                    value = term if value is None else value + term
                start = step * cells + base
                if with_sea:
                    total[128 + start : 128 + start + block, :] = value
                else:
                    outs[run][start : start + block, :] = value.astype(jnp.bfloat16)
        if with_sea:
            for entry in range(sea.shape[0]):
                start = pattern[1, 0, entry] * 128 - first * cells + 128

                @pl.when((start > 0) & (start < span + 128))
                def _():
                    where = pl.ds(pl.multiple_of(start, 16), 128)
                    total[where, :] = total[where, :] + sea[entry]

            outs[run][...] = total[128 : 128 + span, :].astype(jnp.bfloat16)
        place += count + 2


def gelu(v):
    inner = v * (0.7978845608028654 + 0.035677408136300125 * (v * v))
    half = 0.5 * v
    return half + half * jnp.tanh(inner)


def gather_weights_body(chan, up, down, ocean_up, ocean_down, gain, ocean_gain, *refs):
    pieces, (across, back, ocean_across, ocean_back, gains, ocean_gains) = refs[:4], refs[4:]
    hidden, channels = up.shape
    width = channels // 2
    depth, shallow = hidden // 4, ocean_up.shape[0] // 4
    narrow = ocean_down.shape[1] // 2
    own = chan[0] * width
    mine = pl.ds(pl.multiple_of(own, 128), width)
    shape = (channels, channels)
    rows = lax.broadcasted_iota(jnp.int32, shape, 0)
    inside = rows % width
    half = width // 2
    target = jnp.where(inside < half, 2 * inside, 2 * (inside - half) + 1)
    target = target + jnp.where(rows < width, own, width - own)
    order = (target == lax.broadcasted_iota(jnp.int32, shape, 1)).astype(jnp.bfloat16)
    gains[...] = lax.dot_general(
        jnp.broadcast_to(gain[...].reshape(1, channels), (8, channels)),
        order.astype(jnp.float32),
        NT,
        precision=lax.Precision.HIGHEST,
        preferred_element_type=jnp.float32,
    )[0:1]
    for part in range(8):
        at = slice(part * depth, (part + 1) * depth)
        block = up[at, :] if part < 4 else pieces[part - 4][0:depth, 0:channels]
        across[:, at] = lax.dot_general(
            order, block, NT, preferred_element_type=jnp.float32
        ).astype(jnp.bfloat16)
        back[at, :] = down[at, mine] if part < 4 else pieces[part - 4][0:depth, channels : channels + width]
    own = chan[0] * narrow
    mine = pl.ds(pl.multiple_of(own, 128), narrow)
    theirs = pl.ds(pl.multiple_of(narrow - own, 128), narrow)
    wide = ocean_gain[...].reshape(1, 2 * narrow)
    first, second = wide[:, 0:narrow], wide[:, narrow:]
    low = jnp.full((1, narrow), chan[0], jnp.int32) == 0
    ocean_gains[:, 0:narrow] = jnp.where(low, first, second)
    ocean_gains[:, narrow:] = jnp.where(low, second, first)
    count = ocean_up.shape[0]
    ocean_across[0:count, 0:narrow] = ocean_up[:, mine]
    ocean_across[0:count, narrow : 2 * narrow] = ocean_up[:, theirs]
    ocean_back[:, 0:count] = ocean_down[:, mine].T
    parts = []
    for part in range(4):
        for side in range(2):
            start = count + part * shallow + side * (shallow // 2)
            at = slice(start, start + shallow // 2)
            low = slice(depth, depth + shallow // 2)
            base = side * 3 * narrow
            left = pl.multiple_of(base + own, 128)
            right = pl.multiple_of(base + narrow - own, 128)
            ocean_across[at, 0:narrow] = pieces[part][low, pl.ds(left, narrow)]
            ocean_across[at, narrow : 2 * narrow] = pieces[part][low, pl.ds(right, narrow)]
            parts.append(pieces[part][low, base + 2 * narrow : base + 3 * narrow])
    ocean_back[:, count:] = jnp.concatenate(parts, axis=0).T


def atmos_layer_body(own_even, own_odd, other_even, other_odd, gain, across, back, *refs):
    out = refs[-1]
    values = jnp.concatenate([own_even[...], own_odd[...], other_even[...], other_odd[...]], axis=1)
    width = values.shape[1] // 2
    wide = values.astype(jnp.float32)
    squares = jnp.sum(wide * wide, axis=1, keepdims=True)
    inverse = lax.rsqrt(squares * (1.0 / (2 * width)) + 1e-06)
    normed = (wide * inverse * gain[...]).astype(jnp.bfloat16)
    total = jnp.dot(values[:, 0:width], weaver(width), preferred_element_type=jnp.float32)
    step = 512
    for base in range(0, across.shape[1], step):
        at = slice(base, base + step)
        v = jnp.dot(normed, across[:, at], preferred_element_type=jnp.float32)
        total = total + jnp.dot(gelu(v).astype(jnp.bfloat16), back[at, :], preferred_element_type=jnp.float32)
    out[0] = total.astype(jnp.bfloat16)


def flux_remap_body(pattern, slots, blocks, ocean, out, total):
    total[...] = jnp.zeros_like(total)
    group = math.gcd(pattern.shape[2], 8)

    def entries(step, carry):
        found = []
        for index in range(group):
            at = step * group + index
            found.append(
                jnp.dot(slots[pattern[0, 0, at]], blocks[pattern[2, 0, at]], preferred_element_type=jnp.float32)
            )
        for index in range(group):
            tile = pattern[1, 0, step * group + index]
            total[tile] = total[tile] + found[index]
        return carry

    lax.fori_loop(0, pattern.shape[2] // group, entries, 0)
    for tile in range(total.shape[0]):
        lanes = slice(tile * 128, tile * 128 + 128)
        out[:, lanes] = (ocean[:, lanes].astype(jnp.float32) + 0.125 * total[tile]).astype(jnp.bfloat16)


def ocean_layer_body(mask, own, other, gain, across, back, out):
    width = own.shape[0]
    square = (width, width)
    tall = [jnp.broadcast_to(gain[:, k * width : (k + 1) * width], square).T[:, 0:1] for k in range(2)]
    group = math.gcd(mask.shape[0], 4)
    for base in range(0, mask.shape[0], group):
        lanes = slice(base * 128, (base + group) * 128)
        a = own[:, lanes].astype(jnp.float32)
        b = other[:, lanes].astype(jnp.float32)
        squares = jnp.sum(a * a + b * b, axis=0, keepdims=True)
        inverse = lax.rsqrt(squares * (1.0 / (2 * width)) + 1e-06)
        normed = jnp.concatenate([a * inverse * tall[0], b * inverse * tall[1]], axis=0).astype(jnp.bfloat16)
        v = jnp.dot(across[...], normed, preferred_element_type=jnp.float32)
        hidden = gelu(v).astype(jnp.bfloat16)
        delta = jnp.dot(back[...], hidden, preferred_element_type=jnp.float32)
        for tile in range(group):
            inside = slice(tile * 128, tile * 128 + 128)
            keep = mask[base + tile].astype(jnp.float32)
            at = slice((base + tile) * 128, (base + tile + 1) * 128)
            out[:, at] = (a[:, inside] + keep * delta[:, inside]).astype(jnp.bfloat16)


def pack_body(place, up, down, ocean_up, ocean_down, out):
    depth, channels = up.shape
    half, narrow = ocean_up.shape[0] // 2, ocean_down.shape[1]
    out[0:depth, 0:channels] = up[...]
    out[0:depth, channels:] = down[...]
    for side in range(2):
        base, rows = side * 3 * narrow, slice(side * half, (side + 1) * half)
        out[depth:, base : base + 2 * narrow] = ocean_up[rows, :]
        out[depth:, base + 2 * narrow : base + 3 * narrow] = ocean_down[rows, :]


def pack_weights(up, down, ocean_up, ocean_down):
    quarter = lax.axis_index("groups") * 2 + lax.axis_index("pair")
    place = jnp.stack([quarter, 1 - lax.axis_index("chan")])
    depth, shallow = up.shape[0] // 4, ocean_up.shape[0] // 4
    width, narrow = up.shape[1] // 2, ocean_up.shape[1] // 2
    shape = (depth + shallow // 2, 3 * width)
    return pl.pallas_call(
        pack_body,
        grid_spec=pltpu.PrefetchScalarGridSpec(
            num_scalar_prefetch=1,
            grid=(1,),
            in_specs=[
                pl.BlockSpec((depth, 2 * width), lambda _, place: (place[0], 0)),
                pl.BlockSpec((depth, width), lambda _, place: (place[0], place[1])),
                pl.BlockSpec((shallow, 2 * narrow), lambda _, place: (place[0], 0)),
                pl.BlockSpec((shallow, narrow), lambda _, place: (place[0], place[1])),
            ],
            out_specs=pl.BlockSpec(shape, lambda _, place: (0, 0)),
        ),
        out_shape=jax.ShapeDtypeStruct(shape, up.dtype),
        compiler_params=pltpu.CompilerParams(vmem_limit_bytes=60 * 2**20),
    )(place, up, down, ocean_up, ocean_down)


def after(value, *earlier):
    return lax.optimization_barrier((value, *earlier))[0]


def quick_shards(
    atmosphere,
    ocean_state,
    conv_taps,
    atmos_gain,
    atmos_up,
    atmos_down,
    ocean_gain,
    ocean_up,
    ocean_down,
    remap_blocks,
    flux_sends,
    flux_pattern,
    sea_sends,
    sea_pattern,
    ocean_mask,
):
    bf16, f32 = jnp.bfloat16, jnp.float32
    channels, lat_rows, lon_cells = atmosphere.shape
    flux_depth, ocean_cells = ocean_state.shape
    ocean_count = ocean_cells // 128
    hidden = 2 * atmos_up.shape[0]
    ocean_hidden = 2 * ocean_up.shape[0]
    lat_bands = lax.axis_size("lat")
    peers = ("lat", "pair")
    chan = lax.axis_index("chan").reshape(1)
    field = atmosphere.transpose(1, 2, 0)
    taps = conv_taps.T
    sea_rows = sea_pattern.transpose(2, 0, 1)
    flux_rows = flux_pattern.transpose(2, 0, 1)

    sides = local_call(
        sides_body,
        jax.ShapeDtypeStruct((2 * lat_rows, channels), bf16),
        (field, field),
        [
            pl.BlockSpec((lat_rows, 16, channels), lambda _: (0, lon_cells // 16 - 1, 0)),
            pl.BlockSpec((lat_rows, 16, channels), lambda _: (0, 0, 0)),
        ],
        vmem(),
        60,
    )
    sides = lax.ppermute(sides, "pair", SWAP)
    def smooth_rows(odd, runs, field):
        operands, specs, marked = [], [], []
        for first, count in runs:
            halos = []
            for row in range(first - 1, first + count + 1):
                if row < 0 or row >= lat_rows:
                    operands.append((low if row < 0 else high)[None])
                    specs.append(vmem())
                    halos.append(row)
                else:
                    operands.append(field)
                    specs.append(pl.BlockSpec((1, lon_cells, channels), lambda _, row=row: (row, 0, 0)))
            marked.append((first, count, tuple(halos)))
        places = len(operands)
        operands += [sides, taps]
        specs += [vmem(), vmem()]
        scratch = [pltpu.VMEM((places, lon_cells + 16, channels // 2), f32)]
        if odd:
            operands += [sea_rows, sea]
            specs += [smem(), vmem()]
            longest = max(count for _, count in runs)
            scratch.append(pltpu.VMEM((longest * lon_cells + 256, channels // 2), f32))
        return local_call(
            functools.partial(smooth_body, odd, tuple(marked), bool(odd)),
            [jax.ShapeDtypeStruct((count * lon_cells, channels // 2), bf16) for _, count in runs],
            operands,
            specs,
            [vmem() for _ in runs],
            24,
            scratch=scratch,
        )

    edge = lat_rows // 4
    middle = [(edge, lat_rows - 2 * edge)]
    ends_runs = [(0, edge), (lat_rows - edge, edge)]

    def cross(values):
        return [lax.ppermute(value, "chan", SWAP) for value in values]

    evens = smooth_rows(0, middle, field)
    others = cross(evens)
    sea_out = local_call(
        sea_pick_body,
        jax.ShapeDtypeStruct((sea_sends.size, 128, flux_depth), bf16),
        (sea_sends.reshape(1, 1, -1), after(ocean_state, *evens)),
        [smem(), vmem()],
        vmem(),
        60,
    )
    sea_in = lax.all_to_all(sea_out, peers, split_axis=0, concat_axis=0, tiled=True)
    row = jax.ShapeDtypeStruct((lon_cells + 16, channels), bf16)
    messages = local_call(
        edges_body,
        [row, row],
        (after(field, sea_out), field, sides),
        [
            pl.BlockSpec((1, lon_cells, channels), lambda _: (lat_rows - 1, 0, 0)),
            pl.BlockSpec((1, lon_cells, channels), lambda _: (0, 0, 0)),
            vmem(),
        ],
        [vmem()] * 2,
        40,
    )
    low = lax.ppermute(messages[0], "lat", [(i, i + 1) for i in range(lat_bands - 1)])
    high = lax.ppermute(messages[1], "lat", [(i + 1, i) for i in range(lat_bands - 1)])
    packed = pack_weights(after(atmos_up, *messages), atmos_down, ocean_up, ocean_down)
    one = lax.ppermute(packed, "chan", SWAP)
    flux_out = local_call(
        flux_pick_body,
        jax.ShapeDtypeStruct((flux_sends.size, flux_depth, 128), bf16),
        (flux_sends, after(field, packed).reshape(lat_rows * lon_cells, channels)),
        [smem(), vmem()],
        vmem(),
        24,
        scratch=[pltpu.VMEM((lat_rows * lon_cells // 128, flux_depth, 128), bf16)],
    )

    entries = sea_pattern.shape[1]
    sea = local_call(
        sea_products_body,
        jax.ShapeDtypeStruct((entries, 128, flux_depth), f32),
        (sea_rows, sea_in, after(remap_blocks, flux_out)),
        [smem(), vmem(), vmem()],
        vmem(),
        16,
    )
    odds = smooth_rows(1, middle, field)
    others_odd = cross(odds)
    plan = list(zip(middle, evens, odds, others, others_odd))
    flux_in = lax.all_to_all(after(flux_out, low, high, *others, one), peers, split_axis=0, concat_axis=0, tiled=True)
    two = lax.ppermute(after(one, sea), "groups", SWAP)
    ends_even = smooth_rows(0, ends_runs, after(field, *odds))
    others_even = cross(ends_even)
    odds = smooth_rows(1, ends_runs, after(field, *ends_even, one))
    others_odd = cross(odds)
    three, four = lax.ppermute(after(one, *odds), "pair", SWAP), lax.ppermute(after(two, *odds), "pair", SWAP)
    pieces = one, two, three, four
    plan += list(zip(ends_runs, ends_even, odds, others_even, others_odd))

    across, back, ocean_across, ocean_back, gain, gain_ocean = local_call(
        gather_weights_body,
        [
            jax.ShapeDtypeStruct((2 * channels, hidden), bf16),
            jax.ShapeDtypeStruct((hidden, channels), bf16),
            jax.ShapeDtypeStruct((ocean_hidden, 2 * flux_depth), bf16),
            jax.ShapeDtypeStruct((flux_depth, ocean_hidden), bf16),
            jax.ShapeDtypeStruct((1, 2 * channels), f32),
            jax.ShapeDtypeStruct((1, 2 * flux_depth), f32),
        ],
        (chan, after(atmos_up, *odds), atmos_down, ocean_up, ocean_down, atmos_gain, ocean_gain, *pieces),
        [smem()] + [vmem()] * 10,
        [vmem()] * 6,
        32,
    )
    result = None
    for step, ((first, count), *values) in enumerate(plan):
        if step == len(plan) - 1:
            entries = flux_pattern.shape[1]
            ocean_input = local_call(
                flux_remap_body,
                jax.ShapeDtypeStruct((flux_depth, ocean_cells), bf16),
                (flux_rows, flux_in, after(remap_blocks, result), ocean_state),
                [smem(), vmem(), vmem(), vmem()],
                vmem(),
                60,
                scratch=[pltpu.VMEM((ocean_count, flux_depth, 128), f32)],
            )
            ocean_other = lax.ppermute(ocean_input, "chan", SWAP)
            result = after(result, ocean_input)
        operands = [*values, gain, across, back]
        specs = [pl.BlockSpec((lon_cells, channels // 2), lambda step: (step, 0))] * 4 + [vmem()] * 3
        aliases = {}
        if result is not None:
            aliases = {len(operands): 0}
            operands.append(result)
            specs.append(anywhere())
        result = local_call(
            atmos_layer_body,
            jax.ShapeDtypeStruct((lat_rows, lon_cells, channels), bf16),
            operands,
            specs,
            pl.BlockSpec((1, lon_cells, channels), lambda step, first=first: (first + step, 0, 0)),
            24,
            grid=count,
            aliases=aliases,
        )
    ocean_next = local_call(
        ocean_layer_body,
        jax.ShapeDtypeStruct((flux_depth, ocean_cells), bf16),
        (ocean_mask, after(ocean_input, result), ocean_other, gain_ocean, ocean_across, ocean_back),
        [smem()] + [vmem()] * 5,
        vmem(),
        16,
    )
    return result.transpose(2, 0, 1), ocean_next


def solution(mesh):
    in_specs = (
        P("chan", ("groups", "lat"), "pair"),
        P("chan", ("groups", "lat", "pair")),
        P("chan", None),
        P(),
        P("chan", None),
        P("chan", None),
        P(),
        P("chan", None),
        P("chan", None),
        P(),
        P(("lat", "pair"), None, None),
        P(("lat", "pair"), None, None),
        P(("lat", "pair"), None, None),
        P(("lat", "pair"), None, None),
        P(("lat", "pair")),
    )
    out_specs = (P("chan", ("groups", "lat"), "pair"), P("chan", ("groups", "lat", "pair")))
    paired = all(mesh.shape[axis] == 2 for axis in ("groups", "chan", "pair")) and mesh.shape["lat"] > 2
    body = quick_shards if paired else shards
    return jax.shard_map(body, mesh=mesh, in_specs=in_specs, out_specs=out_specs, check_vma=False)
```

```python
import functools
import math

import jax
import jax.numpy as jnp
from jax import lax
from jax.experimental import pallas as pl
from jax.experimental.pallas import tpu as pltpu
from jax.sharding import PartitionSpec as P


def padded_2(block, sides, width):
    for axis, dim in sides:
        count = lax.axis_size(axis)
        forward = [(i, i + 1) for i in range(count - 1)]
        forward.append((count - 1, 0))
        backward = [(target, source) for source, target in forward]
        low = lax.ppermute(
            lax.slice_in_dim(block, block.shape[dim] - width, None, axis=dim), axis, forward
        )
        high = lax.ppermute(lax.slice_in_dim(block, 0, width, axis=dim), axis, backward)
        block = jnp.concatenate([low, block, high], axis=dim)
    return block


def remap_tiles(received, pattern, blocks, tile_count, factor):
    flux_depth = received.shape[0]
    entries = pattern.shape[0]
    group_size = math.gcd(entries, 64)
    grouped = pattern.reshape(entries // group_size, group_size, 3)
    targets = jnp.arange(tile_count, dtype=jnp.int32)

    def add_group(running, entry_rows):
        picked = jnp.take(received, entry_rows[:, 0], axis=1)
        weights = jnp.take(blocks, entry_rows[:, 2], axis=0)
        products = jnp.einsum("kgi,gij->kgj", picked, weights, preferred_element_type=jnp.float32)
        onehot = (entry_rows[:, 1][:, None] == targets[None, :]).astype(jnp.float32)
        return (running + jnp.einsum("kgj,gt->ktj", products, onehot), None)

    initial = jnp.zeros((flux_depth, tile_count, 128), jnp.float32)
    summed, _ = lax.scan(add_group, initial, grouped)
    return summed * factor


def normalize(values, channel_gain):
    widened = values.astype(jnp.float32)
    inverse = lax.rsqrt(jnp.mean(widened * widened, axis=0, keepdims=True) + 1e-06)
    return (widened * inverse * channel_gain[:, None]).astype(jnp.bfloat16)


def shards(
    atmosphere,
    ocean_state,
    conv_taps,
    atmos_gain,
    atmos_up,
    atmos_down,
    ocean_gain,
    ocean_up,
    ocean_down,
    remap_blocks,
    flux_sends,
    flux_pattern,
    sea_sends,
    sea_pattern,
    ocean_mask,
):
    lat_bands = lax.axis_size("lat")
    halves = lax.axis_size("pair")
    peer_count = lat_bands * halves
    channels, lat_rows, lon_cells = atmosphere.shape
    flux_depth, ocean_cells = ocean_state.shape
    atmos_count = lat_rows * lon_cells // 128
    ocean_count = ocean_cells // 128
    flux_slots = flux_sends.shape[2]
    sea_slots = sea_sends.shape[2]
    flux_tiles = atmosphere[0::2].reshape(flux_depth, atmos_count, 128)
    ocean_tiles = ocean_state.reshape(flux_depth, ocean_count, 128)
    flux_out = jnp.take(flux_tiles, flux_sends[0].reshape(-1), axis=1)
    sea_out = jnp.take(ocean_tiles, sea_sends[0].reshape(-1), axis=1)
    flux_in, sea_in = (
        lax.all_to_all(
            flux_out.reshape(flux_depth, peer_count, flux_slots, 128),
            ("lat", "pair"),
            split_axis=1,
            concat_axis=1,
            tiled=True,
        ),
        lax.all_to_all(
            sea_out.reshape(flux_depth, peer_count, sea_slots, 128),
            ("lat", "pair"),
            split_axis=1,
            concat_axis=1,
            tiled=True,
        ),
    )
    flux_in = flux_in.reshape(flux_depth, peer_count * flux_slots, 128)
    sea_in = sea_in.reshape(flux_depth, peer_count * sea_slots, 128)
    flux_ocean = remap_tiles(flux_in, flux_pattern[0], remap_blocks, ocean_count, 0.125)
    sea_atmos = remap_tiles(sea_in, sea_pattern[0], remap_blocks, atmos_count, 1.0)
    ocean_input = (
        ocean_state.astype(jnp.float32) + flux_ocean.reshape(flux_depth, ocean_cells)
    ).astype(jnp.bfloat16)
    padded = padded_2(atmosphere, (("lat", 1), ("pair", 2)), 1)
    lat_index = lax.axis_index("lat")
    edge_rows = jnp.arange(lat_rows + 2)
    row_keep = ((edge_rows > 0) | (lat_index > 0)) & (
        (edge_rows < lat_rows + 1) | (lat_index < lat_bands - 1)
    )
    padded = padded.astype(jnp.float32) * row_keep.astype(jnp.float32)[None, :, None]
    tap_table = conv_taps.astype(jnp.float32)
    smooth = jnp.zeros((channels, lat_rows, lon_cells), jnp.float32)
    for row_step in range(3):
        for col_step in range(3):
            smooth = (
                smooth
                + tap_table[:, 3 * row_step + col_step][:, None, None]
                * padded[:, row_step : row_step + lat_rows, col_step : col_step + lon_cells]
            )
    combined = atmosphere.astype(jnp.float32) + smooth
    combined = combined.at[1::2].add(sea_atmos.reshape(flux_depth, lat_rows, lon_cells))
    atmos_input = combined.astype(jnp.bfloat16)
    atmos_cells, ocean_part = (
        lax.all_to_all(
            atmos_input.reshape(channels, lat_rows * lon_cells),
            "chan",
            split_axis=1,
            concat_axis=0,
            tiled=True,
        ),
        lax.all_to_all(ocean_input, "chan", split_axis=1, concat_axis=0, tiled=True),
    )
    atmos_normed = normalize(atmos_cells, atmos_gain)
    ocean_normed = normalize(ocean_part, ocean_gain)
    up_rows = lax.all_gather(atmos_up, "chan", axis=0, tiled=True)
    down_rows = lax.all_gather(atmos_down, "chan", axis=0, tiled=True)
    ocean_up_rows = lax.all_gather(ocean_up, "chan", axis=0, tiled=True)
    ocean_down_rows = lax.all_gather(ocean_down, "chan", axis=0, tiled=True)
    hidden = jax.nn.gelu(jnp.dot(up_rows, atmos_normed, preferred_element_type=jnp.float32)).astype(
        jnp.bfloat16
    )
    atmos_sum = lax.dot_general(
        down_rows, hidden, (((0,), (0,)), ((), ())), preferred_element_type=jnp.float32
    )
    ocean_hidden = jax.nn.gelu(
        jnp.dot(ocean_up_rows, ocean_normed, preferred_element_type=jnp.float32)
    ).astype(jnp.bfloat16)
    ocean_sum = lax.dot_general(
        ocean_down_rows, ocean_hidden, (((0,), (0,)), ((), ())), preferred_element_type=jnp.float32
    )
    ocean_stretch = ocean_part.shape[1]
    mask_cells = jnp.repeat(ocean_mask.astype(jnp.float32), 128)
    mask_cells = lax.dynamic_slice_in_dim(
        mask_cells, lax.axis_index("chan") * ocean_stretch, ocean_stretch
    )
    atmos_after = (atmos_cells.astype(jnp.float32) + atmos_sum).astype(jnp.bfloat16)
    ocean_after = (ocean_part.astype(jnp.float32) + mask_cells[None, :] * ocean_sum).astype(
        jnp.bfloat16
    )
    atmos_back, ocean_back = (
        lax.all_to_all(atmos_after, "chan", split_axis=0, concat_axis=1, tiled=True),
        lax.all_to_all(ocean_after, "chan", split_axis=0, concat_axis=1, tiled=True),
    )
    return (atmos_back.reshape(channels, lat_rows, lon_cells), ocean_back)


SWAP = [(0, 1), (1, 0)]
NT = (((1,), (1,)), ((), ()))
TN = (((0,), (0,)), ((), ()))


def vmem():
    return pl.BlockSpec(memory_space=pltpu.VMEM)


def smem():
    return pl.BlockSpec(memory_space=pltpu.SMEM)


def anywhere():
    return pl.BlockSpec(memory_space=pl.ANY)


def local_call(
    body, out_shape, operands, in_specs, out_specs, limit, grid=1, scratch=(), aliases=None
):
    return pl.pallas_call(
        body,
        grid=(grid,),
        out_shape=out_shape,
        in_specs=in_specs,
        out_specs=out_specs,
        scratch_shapes=list(scratch),
        input_output_aliases=aliases or {},
        compiler_params=pltpu.CompilerParams(vmem_limit_bytes=limit * 2**20),
        cost_estimate=pl.CostEstimate(flops=1, bytes_accessed=1, transcendentals=0),
    )(*operands)


def picker(channels, odd):
    shape = (channels, channels // 2)
    rows = lax.broadcasted_iota(jnp.int32, shape, 0)
    return (rows == 2 * lax.broadcasted_iota(jnp.int32, shape, 1) + odd).astype(jnp.bfloat16)


def weaver(channels):
    shape = (channels, channels)
    rows = lax.broadcasted_iota(jnp.int32, shape, 0)
    half = channels // 2
    target = jnp.where(rows < half, 2 * rows, 2 * (rows - half) + 1)
    return (target == lax.broadcasted_iota(jnp.int32, shape, 1)).astype(jnp.bfloat16)


def sea_pick_body(sends, ocean, out):
    for entry in range(out.shape[0]):
        at = pl.multiple_of(sends[0, 0, entry] * 128, 128)
        out[entry] = ocean[:, pl.ds(at, 128)].T


def sides_body(right, left, sides):
    for row in range(right.shape[0]):
        sides[2 * row : 2 * row + 1, :] = right[row, right.shape[1] - 1 : right.shape[1], :]
        sides[2 * row + 1 : 2 * row + 2, :] = left[row, 0:1, :]


def edges_body(last, first, sides, *outs):
    cells = last.shape[1]
    for out, row, at in ((outs[0], last, sides.shape[0] - 2), (outs[1], first, 0)):
        out[0:cells, :] = row[0]
        out[cells : cells + 2, :] = sides[at : at + 2, :]
        out[cells + 2 : cells + 16, :] = jnp.zeros((14, row.shape[2]), jnp.bfloat16)


def flux_pick_body(sends, cells, out, even):
    _, count, cap = sends.shape
    take = picker(cells.shape[1], 0)

    def one_tile(tile, carry):
        at = pl.multiple_of(tile * 128, 128)
        values = jnp.dot(cells[pl.ds(at, 128), :], take, preferred_element_type=jnp.float32)
        even[tile] = values.T.astype(jnp.bfloat16)
        return carry

    lax.fori_loop(0, even.shape[0], one_tile, 0, unroll=5)

    def one_peer(peer, carry):
        for slot in range(cap):
            out[peer * cap + slot] = even[sends[0, peer, slot]]
        return carry

    lax.fori_loop(0, count, one_peer, 0, unroll=2)


def sea_products_body(pattern, slots, blocks, out):
    def entry(index, carry):
        out[index] = lax.dot_general(
            blocks[pattern[2, 0, index]],
            slots[pattern[0, 0, index]],
            TN,
            preferred_element_type=jnp.float32,
        )
        return carry

    lax.fori_loop(0, out.shape[0], entry, 0, unroll=8)


def smooth_body(odd, runs, with_sea, *refs):
    places = sum(count + 2 for _, count, _ in runs)
    rows, rest = refs[:places], refs[places:]
    sides, taps = rest[:2]
    pattern, sea = rest[2:4] if with_sea else (None, None)
    outs = rest[4:-2] if with_sea else rest[2:-1]
    padded = rest[-2] if with_sea else rest[-1]
    total = rest[-1]
    cells, channels = rows[0].shape[1], rows[0].shape[2]
    cells = min(row.shape[1] for row in rows)
    take = picker(channels, odd)
    edges = jnp.dot(sides[...], take, preferred_element_type=jnp.float32)
    scale = jnp.dot(taps[...], take, preferred_element_type=jnp.float32)
    scale = [scale[k : k + 1] + (1.0 if k == 4 else 0.0) for k in range(9)]
    place = 0
    for run, (first, count, halos) in enumerate(runs):
        span = count * cells
        for step in range(count + 2):
            row = first - 1 + step
            values = rows[place + step][0, 0 : cells + 16] if row in halos else rows[place + step][0]
            values = jnp.dot(values, take, preferred_element_type=jnp.float32)
            if row in halos:
                left, right = values[cells : cells + 1], values[cells + 1 : cells + 2]
            else:
                left, right = edges[2 * row : 2 * row + 1], edges[2 * row + 1 : 2 * row + 2]
            padded[place + step, 8 : 8 + cells, :] = values[0:cells]
            padded[place + step, 7:8, :] = left
            padded[place + step, 8 + cells : 9 + cells, :] = right
        block = 144 if cells % 144 == 0 else 16
        for step in range(count):
            for base in range(0, cells, block):
                value = None
                for k in range(9):
                    start = 7 + base + k % 3
                    term = scale[k] * padded[place + step + k // 3, start : start + block, :]
                    value = term if value is None else value + term
                start = step * cells + base
                if with_sea:
                    total[128 + start : 128 + start + block, :] = value
                else:
                    outs[run][start : start + block, :] = value.astype(jnp.bfloat16)
        if with_sea:
            for entry in range(sea.shape[0]):
                start = pattern[1, 0, entry] * 128 - first * cells + 128

                @pl.when((start > 0) & (start < span + 128))
                def _():
                    where = pl.ds(pl.multiple_of(start, 16), 128)
                    total[where, :] = total[where, :] + sea[entry]

            outs[run][...] = total[128 : 128 + span, :].astype(jnp.bfloat16)
        place += count + 2


def gelu(v):
    inner = v * (0.7978845608028654 + 0.035677408136300125 * (v * v))
    half = 0.5 * v
    return half + half * jnp.tanh(inner)


def gather_weights_body(chan, up, down, ocean_up, ocean_down, gain, ocean_gain, *refs):
    pieces, (across, back, ocean_across, ocean_back, gains, ocean_gains) = refs[:4], refs[4:]
    hidden, channels = up.shape
    width = channels // 2
    depth, shallow = hidden // 4, ocean_up.shape[0] // 4
    narrow = ocean_down.shape[1] // 2
    own = chan[0] * width
    mine = pl.ds(pl.multiple_of(own, 128), width)
    shape = (channels, channels)
    rows = lax.broadcasted_iota(jnp.int32, shape, 0)
    inside = rows % width
    half = width // 2
    target = jnp.where(inside < half, 2 * inside, 2 * (inside - half) + 1)
    target = target + jnp.where(rows < width, own, width - own)
    order = (target == lax.broadcasted_iota(jnp.int32, shape, 1)).astype(jnp.bfloat16)
    gains[...] = lax.dot_general(
        jnp.broadcast_to(gain[...].reshape(1, channels), (8, channels)),
        order.astype(jnp.float32),
        NT,
        precision=lax.Precision.HIGHEST,
        preferred_element_type=jnp.float32,
    )[0:1]
    for part in range(8):
        at = slice(part * depth, (part + 1) * depth)
        block = up[at, :] if part < 4 else pieces[part - 4][0:depth, 0:channels]
        across[:, at] = lax.dot_general(
            order, block, NT, preferred_element_type=jnp.float32
        ).astype(jnp.bfloat16)
        back[at, :] = down[at, mine] if part < 4 else pieces[part - 4][0:depth, channels : channels + width]
    own = chan[0] * narrow
    mine = pl.ds(pl.multiple_of(own, 128), narrow)
    theirs = pl.ds(pl.multiple_of(narrow - own, 128), narrow)
    wide = ocean_gain[...].reshape(1, 2 * narrow)
    first, second = wide[:, 0:narrow], wide[:, narrow:]
    low = jnp.full((1, narrow), chan[0], jnp.int32) == 0
    ocean_gains[:, 0:narrow] = jnp.where(low, first, second)
    ocean_gains[:, narrow:] = jnp.where(low, second, first)
    count = ocean_up.shape[0]
    ocean_across[0:count, 0:narrow] = ocean_up[:, mine]
    ocean_across[0:count, narrow : 2 * narrow] = ocean_up[:, theirs]
    ocean_back[:, 0:count] = ocean_down[:, mine].T
    parts = []
    for part in range(4):
        for side in range(2):
            start = count + part * shallow + side * (shallow // 2)
            at = slice(start, start + shallow // 2)
            low = slice(depth, depth + shallow // 2)
            base = side * 3 * narrow
            left = pl.multiple_of(base + own, 128)
            right = pl.multiple_of(base + narrow - own, 128)
            ocean_across[at, 0:narrow] = pieces[part][low, pl.ds(left, narrow)]
            ocean_across[at, narrow : 2 * narrow] = pieces[part][low, pl.ds(right, narrow)]
            parts.append(pieces[part][low, base + 2 * narrow : base + 3 * narrow])
    ocean_back[:, count:] = jnp.concatenate(parts, axis=0).T


def atmos_layer_body(own_even, own_odd, other_even, other_odd, gain, across, back, *refs):
    out = refs[-1]
    values = jnp.concatenate([own_even[...], own_odd[...], other_even[...], other_odd[...]], axis=1)
    width = values.shape[1] // 2
    wide = values.astype(jnp.float32)
    squares = jnp.sum(wide * wide, axis=1, keepdims=True)
    inverse = lax.rsqrt(squares * (1.0 / (2 * width)) + 1e-06)
    normed = (wide * inverse * gain[...]).astype(jnp.bfloat16)
    total = jnp.dot(values[:, 0:width], weaver(width), preferred_element_type=jnp.float32)
    step = 512
    for base in range(0, across.shape[1], step):
        at = slice(base, base + step)
        v = jnp.dot(normed, across[:, at], preferred_element_type=jnp.float32)
        total = total + jnp.dot(gelu(v).astype(jnp.bfloat16), back[at, :], preferred_element_type=jnp.float32)
    out[0] = total.astype(jnp.bfloat16)


def slot_uses_body(pattern, uses):
    def clear(slot, carry):
        uses[0, slot] = -1
        return carry

    def note(entry, carry):
        slot = pattern[0, 0, entry]
        uses[jnp.where(uses[0, slot] >= 0, 1, 0), slot] = entry
        return carry

    lax.fori_loop(0, uses.shape[1], clear, 0, unroll=8)
    lax.fori_loop(0, pattern.shape[2], note, 0, unroll=8)


def flux_remap_body(pattern, uses, slots, blocks, ocean, out, total):
    total[...] = jnp.zeros_like(total)
    group = math.gcd(slots.shape[0], 8)

    def some_slots(step, carry):
        found = []
        for index in range(group):
            slot = step * group + index
            wide = jnp.concatenate(
                [blocks[pattern[2, 0, uses[0, slot]]], blocks[pattern[2, 0, uses[1, slot]]]], axis=1
            )
            found.append(jnp.dot(slots[slot], wide, preferred_element_type=jnp.float32))
        for index in range(group):
            for use in range(2):
                tile = pattern[1, 0, uses[use, step * group + index]]
                total[tile] = total[tile] + found[index][:, use * 128 : use * 128 + 128]
        return carry

    lax.fori_loop(0, slots.shape[0] // group, some_slots, 0)
    for tile in range(total.shape[0]):
        lanes = slice(tile * 128, tile * 128 + 128)
        out[:, lanes] = (ocean[:, lanes].astype(jnp.float32) + 0.125 * total[tile]).astype(jnp.bfloat16)


def ocean_layer_body(mask, own, other, gain, across, back, out):
    width = own.shape[0]
    square = (width, width)
    tall = [jnp.broadcast_to(gain[:, k * width : (k + 1) * width], square).T[:, 0:1] for k in range(2)]
    group = math.gcd(mask.shape[0], 4)
    for base in range(0, mask.shape[0], group):
        lanes = slice(base * 128, (base + group) * 128)
        a = own[:, lanes].astype(jnp.float32)
        b = other[:, lanes].astype(jnp.float32)
        squares = jnp.sum(a * a + b * b, axis=0, keepdims=True)
        inverse = lax.rsqrt(squares * (1.0 / (2 * width)) + 1e-06)
        normed = jnp.concatenate([a * inverse * tall[0], b * inverse * tall[1]], axis=0).astype(jnp.bfloat16)
        v = jnp.dot(across[...], normed, preferred_element_type=jnp.float32)
        hidden = gelu(v).astype(jnp.bfloat16)
        delta = jnp.dot(back[...], hidden, preferred_element_type=jnp.float32)
        for tile in range(group):
            inside = slice(tile * 128, tile * 128 + 128)
            keep = mask[base + tile].astype(jnp.float32)
            at = slice((base + tile) * 128, (base + tile + 1) * 128)
            out[:, at] = (a[:, inside] + keep * delta[:, inside]).astype(jnp.bfloat16)


def pack_body(quarter, other, up, down, ocean_up, ocean_down, out):
    depth, channels = up.shape
    half, narrow = ocean_up.shape[0] // 2, ocean_down.shape[1]
    out[0:depth, 0:channels] = up[...]
    out[0:depth, channels:] = down[...]
    for side in range(2):
        base, rows = side * 3 * narrow, slice(side * half, (side + 1) * half)
        out[depth:, base : base + 2 * narrow] = ocean_up[rows, :]
        out[depth:, base + 2 * narrow : base + 3 * narrow] = ocean_down[rows, :]


def pack_weights(up, down, ocean_up, ocean_down):
    quarter = (lax.axis_index("groups") * 2 + lax.axis_index("pair")).reshape(1)
    other = (1 - lax.axis_index("chan")).reshape(1)
    depth, shallow = up.shape[0] // 4, ocean_up.shape[0] // 4
    width, narrow = up.shape[1] // 2, ocean_up.shape[1] // 2
    shape = (depth + shallow // 2, 3 * width)
    return pl.pallas_call(
        pack_body,
        grid_spec=pltpu.PrefetchScalarGridSpec(
            num_scalar_prefetch=2,
            grid=(1,),
            in_specs=[
                pl.BlockSpec((depth, 2 * width), lambda _, quarter, other: (quarter[0], 0)),
                pl.BlockSpec((depth, width), lambda _, quarter, other: (quarter[0], other[0])),
                pl.BlockSpec((shallow, 2 * narrow), lambda _, quarter, other: (quarter[0], 0)),
                pl.BlockSpec((shallow, narrow), lambda _, quarter, other: (quarter[0], other[0])),
            ],
            out_specs=pl.BlockSpec(shape, lambda _, quarter, other: (0, 0)),
        ),
        out_shape=jax.ShapeDtypeStruct(shape, up.dtype),
        compiler_params=pltpu.CompilerParams(vmem_limit_bytes=60 * 2**20),
    )(quarter, other, up, down, ocean_up, ocean_down)


def after(value, *earlier):
    return lax.optimization_barrier((value, *earlier))[0]


def quick_shards(
    atmosphere,
    ocean_state,
    conv_taps,
    atmos_gain,
    atmos_up,
    atmos_down,
    ocean_gain,
    ocean_up,
    ocean_down,
    remap_blocks,
    flux_sends,
    flux_pattern,
    sea_sends,
    sea_pattern,
    ocean_mask,
):
    bf16, f32 = jnp.bfloat16, jnp.float32
    channels, lat_rows, lon_cells = atmosphere.shape
    flux_depth, ocean_cells = ocean_state.shape
    ocean_count = ocean_cells // 128
    hidden = 2 * atmos_up.shape[0]
    ocean_hidden = 2 * ocean_up.shape[0]
    lat_bands = lax.axis_size("lat")
    peers = ("lat", "pair")
    chan = lax.axis_index("chan").reshape(1)
    field = atmosphere.transpose(1, 2, 0)
    taps = conv_taps.T
    sea_rows = sea_pattern.transpose(2, 0, 1)
    flux_rows = flux_pattern.transpose(2, 0, 1)

    sides = local_call(
        sides_body,
        jax.ShapeDtypeStruct((2 * lat_rows, channels), bf16),
        (field, field),
        [
            pl.BlockSpec((lat_rows, 16, channels), lambda _: (0, lon_cells // 16 - 1, 0)),
            pl.BlockSpec((lat_rows, 16, channels), lambda _: (0, 0, 0)),
        ],
        vmem(),
        60,
    )
    sides = lax.ppermute(sides, "pair", SWAP)
    def smooth_rows(odd, runs, field):
        operands, specs, marked = [], [], []
        for first, count in runs:
            halos = []
            for row in range(first - 1, first + count + 1):
                if row < 0 or row >= lat_rows:
                    operands.append((low if row < 0 else high)[None])
                    specs.append(vmem())
                    halos.append(row)
                else:
                    operands.append(field)
                    specs.append(pl.BlockSpec((1, lon_cells, channels), lambda _, row=row: (row, 0, 0)))
            marked.append((first, count, tuple(halos)))
        places = len(operands)
        operands += [sides, taps]
        specs += [vmem(), vmem()]
        scratch = [pltpu.VMEM((places, lon_cells + 16, channels // 2), f32)]
        if odd:
            operands += [sea_rows, sea]
            specs += [smem(), vmem()]
            longest = max(count for _, count in runs)
            scratch.append(pltpu.VMEM((longest * lon_cells + 256, channels // 2), f32))
        return local_call(
            functools.partial(smooth_body, odd, tuple(marked), bool(odd)),
            [jax.ShapeDtypeStruct((count * lon_cells, channels // 2), bf16) for _, count in runs],
            operands,
            specs,
            [vmem() for _ in runs],
            24,
            scratch=scratch,
        )

    edge = lat_rows // 4
    middle = [(edge, lat_rows - 2 * edge)]
    ends_runs = [(0, edge), (lat_rows - edge, edge)]

    def cross(values):
        return [lax.ppermute(value, "chan", SWAP) for value in values]

    evens = smooth_rows(0, middle, field)
    others = cross(evens)
    sea_out = local_call(
        sea_pick_body,
        jax.ShapeDtypeStruct((sea_sends.size, 128, flux_depth), bf16),
        (sea_sends.reshape(1, 1, -1), after(ocean_state, *evens)),
        [smem(), vmem()],
        vmem(),
        60,
    )
    sea_in = lax.all_to_all(sea_out, peers, split_axis=0, concat_axis=0, tiled=True)
    row = jax.ShapeDtypeStruct((lon_cells + 16, channels), bf16)
    messages = local_call(
        edges_body,
        [row, row],
        (after(field, sea_out), field, sides),
        [
            pl.BlockSpec((1, lon_cells, channels), lambda _: (lat_rows - 1, 0, 0)),
            pl.BlockSpec((1, lon_cells, channels), lambda _: (0, 0, 0)),
            vmem(),
        ],
        [vmem()] * 2,
        40,
    )
    low = lax.ppermute(messages[0], "lat", [(i, i + 1) for i in range(lat_bands - 1)])
    high = lax.ppermute(messages[1], "lat", [(i + 1, i) for i in range(lat_bands - 1)])
    packed = pack_weights(after(atmos_up, *messages), atmos_down, ocean_up, ocean_down)
    one = lax.ppermute(packed, "chan", SWAP)
    flux_out = local_call(
        flux_pick_body,
        jax.ShapeDtypeStruct((flux_sends.size, flux_depth, 128), bf16),
        (flux_sends, after(field, packed).reshape(lat_rows * lon_cells, channels)),
        [smem(), vmem()],
        vmem(),
        24,
        scratch=[pltpu.VMEM((lat_rows * lon_cells // 128, flux_depth, 128), bf16)],
    )

    entries = sea_pattern.shape[1]
    sea = local_call(
        sea_products_body,
        jax.ShapeDtypeStruct((entries, 128, flux_depth), f32),
        (sea_rows, sea_in, after(remap_blocks, flux_out)),
        [smem(), vmem(), vmem()],
        vmem(),
        16,
    )
    odds = smooth_rows(1, middle, field)
    others_odd = cross(odds)
    plan = list(zip(middle, evens, odds, others, others_odd))
    flux_in = lax.all_to_all(after(flux_out, low, high, *others, one), peers, split_axis=0, concat_axis=0, tiled=True)
    two = lax.ppermute(after(one, sea), "groups", SWAP)
    ends_even = smooth_rows(0, ends_runs, after(field, *odds))
    others_even = cross(ends_even)
    odds = smooth_rows(1, ends_runs, after(field, *ends_even, one))
    others_odd = cross(odds)
    three, four = lax.ppermute(after(one, *odds), "pair", SWAP), lax.ppermute(after(two, *odds), "pair", SWAP)
    pieces = one, two, three, four
    plan += list(zip(ends_runs, ends_even, odds, others_even, others_odd))

    across, back, ocean_across, ocean_back, gain, gain_ocean = local_call(
        gather_weights_body,
        [
            jax.ShapeDtypeStruct((2 * channels, hidden), bf16),
            jax.ShapeDtypeStruct((hidden, channels), bf16),
            jax.ShapeDtypeStruct((ocean_hidden, 2 * flux_depth), bf16),
            jax.ShapeDtypeStruct((flux_depth, ocean_hidden), bf16),
            jax.ShapeDtypeStruct((1, 2 * channels), f32),
            jax.ShapeDtypeStruct((1, 2 * flux_depth), f32),
        ],
        (chan, after(atmos_up, *odds), atmos_down, ocean_up, ocean_down, atmos_gain, ocean_gain, *pieces),
        [smem()] + [vmem()] * 10,
        [vmem()] * 6,
        32,
    )
    result = None
    for step, ((first, count), *values) in enumerate(plan):
        if step == 1:
            uses = local_call(
                slot_uses_body,
                jax.ShapeDtypeStruct((2, flux_sends.shape[1] * flux_sends.shape[2]), jnp.int32),
                (after(flux_rows, result),),
                [smem()],
                smem(),
                8,
            )
            result = after(result, uses)
        if step == len(plan) - 1:
            entries = flux_pattern.shape[1]
            ocean_input = local_call(
                flux_remap_body,
                jax.ShapeDtypeStruct((flux_depth, ocean_cells), bf16),
                (flux_rows, uses, flux_in, after(remap_blocks, result), ocean_state),
                [smem(), smem(), vmem(), vmem(), vmem()],
                vmem(),
                60,
                scratch=[pltpu.VMEM((ocean_count, flux_depth, 128), f32)],
            )
            ocean_other = lax.ppermute(ocean_input, "chan", SWAP)
            result = after(result, ocean_input)
        operands = [*values, gain, across, back]
        specs = [pl.BlockSpec((lon_cells, channels // 2), lambda step: (step, 0))] * 4 + [vmem()] * 3
        aliases = {}
        if result is not None:
            aliases = {len(operands): 0}
            operands.append(result)
            specs.append(anywhere())
        result = local_call(
            atmos_layer_body,
            jax.ShapeDtypeStruct((lat_rows, lon_cells, channels), bf16),
            operands,
            specs,
            pl.BlockSpec((1, lon_cells, channels), lambda step, first=first: (first + step, 0, 0)),
            24,
            grid=count,
            aliases=aliases,
        )
    ocean_next = local_call(
        ocean_layer_body,
        jax.ShapeDtypeStruct((flux_depth, ocean_cells), bf16),
        (ocean_mask, after(ocean_input, result), ocean_other, gain_ocean, ocean_across, ocean_back),
        [smem()] + [vmem()] * 5,
        vmem(),
        16,
    )
    return result.transpose(2, 0, 1), ocean_next


def solution(mesh):
    in_specs = (
        P("chan", ("groups", "lat"), "pair"),
        P("chan", ("groups", "lat", "pair")),
        P("chan", None),
        P(),
        P("chan", None),
        P("chan", None),
        P(),
        P("chan", None),
        P("chan", None),
        P(),
        P(("lat", "pair"), None, None),
        P(("lat", "pair"), None, None),
        P(("lat", "pair"), None, None),
        P(("lat", "pair"), None, None),
        P(("lat", "pair")),
    )
    out_specs = (P("chan", ("groups", "lat"), "pair"), P("chan", ("groups", "lat", "pair")))
    paired = all(mesh.shape[axis] == 2 for axis in ("groups", "chan", "pair")) and mesh.shape["lat"] > 2
    body = quick_shards if paired else shards
    return jax.shard_map(body, mesh=mesh, in_specs=in_specs, out_specs=out_specs, check_vma=False)
```
